32 devices in a mesh: section: 4 (over x, core), dp: 8 (over z, y).
Axes of the slice: x: 2, y: 2, z: 4, core: 2. Of those that a mesh axis runs over, the one named last changes fastest.
Arguments:
- source: bfloat16 [32, 64, 1024], P('dp'), may hold values from -6 to 6
- target: bfloat16 [32, 64, 1024], P('dp'), may hold values from -6 to 6
- directions: int32 [32], P('dp'), may hold values from 0 to 15
- source_lengths: int32 [32], P('dp'), may hold values from 16 to 64, as said below
- target_lengths: int32 [32], P('dp'), may hold values from 16 to 64, as said below
- attn_in: bfloat16 [4, 1024, 3072], P('section', 'dp'), may hold values from -0.1875 to 0.1875
- attn_out: bfloat16 [4, 1024, 1024], P('section', 'dp'), may hold values from -0.75 to 0.75
- ffn_in: bfloat16 [4, 1024, 4096], P('section', 'dp'), may hold values from -0.1875 to 0.1875
- ffn_out: bfloat16 [4, 4096, 1024], P('section', 'dp'), may hold values from -0.09375 to 0.09375
- cross_weight: bfloat16 [4, 1024, 4096], P('section', 'dp')
- norm_gain: bfloat16 [4, 2, 1024], P('section'), may hold values from 0.25 to 1.75
- norm_bias: bfloat16 [4, 2, 1024], P('section'), may hold values from -4 to 4
- cross_norm: bfloat16 [4, 2, 1024], P('section')
- dir_table: float32 [16, 1024], replicated, may hold values from -6 to 6
- cotangent: bfloat16 [32, 64, 1024], P('dp'), may hold values from -6 to 6
Outputs:
- section_out: bfloat16 [4, 32, 64, 1024], P('section', 'dp')
- section_in_grad: bfloat16 [4, 32, 64, 1024], P('section', 'dp')
- attn_in_grad: float32 [4, 1024, 3072], P('section', 'dp')
- attn_out_grad: float32 [4, 1024, 1024], P('section', 'dp')
- ffn_in_grad: float32 [4, 1024, 4096], P('section', 'dp')
- ffn_out_grad: float32 [4, 4096, 1024], P('section', 'dp')
- cross_weight_grad: float32 [4, 1024, 4096], P('section', 'dp')
- norm_gain_grad: float32 [4, 2, 1024], P('section', None, 'dp')
- norm_bias_grad: float32 [4, 2, 1024], P('section', None, 'dp')
- cross_norm_grad: float32 [4, 2, 1024], P('section', None, 'dp')
- dir_table_grad: float32 [16, 1024], P('section', 'dp')
The draws below stay inside these ranges and needn't reach their ends.
Inputs may be any that keep to these rules, and one draw needn't show every extreme that they name: `source_lengths`: the shortest and the longest source sentence each occur in every draw. `target_lengths`: the shortest and the longest target sentence each occur in every draw.
All inputs are finite; a program needn't handle non-finite values.
Results may differ from the reference program's by a relative error of at most 0.023.
Values may be sent and summed in bfloat16 or wider, within the bound.
A program may use at most 320 MiB of HBM per device.

```python
import math
import jax
import jax.numpy as jnp
import numpy as np
from jax import lax

D = 1024
HEADS = 16
FF = 4096
SEQ = 64
MICRO = 4
NDIR = 16
PAIRS = 32
N_SECTION = 4
N_DP = 8


def draw_lengths(key, lowest):
    first_key, second_key, third_key = jax.random.split(key, 3)
    drawn = jax.random.randint(first_key, (PAIRS,), lowest, SEQ + 1)
    longest = jax.random.randint(second_key, (), 0, PAIRS)
    shortest = (longest + 1 + jax.random.randint(third_key, (), 0, PAIRS - 1)) % PAIRS
    places = jnp.arange(PAIRS)
    drawn = jnp.where(places == longest, SEQ, drawn)
    return jnp.where(places == shortest, lowest, drawn).astype(jnp.int32)


def draw_source_lengths(key, part):
    key = jax.random.fold_in(key, 3)
    return draw_lengths(key, SEQ // 4)


def draw_target_lengths(key, part):
    key = jax.random.fold_in(key, 5)
    return draw_lengths(key, SEQ // 4)


def draw_cross_weight(key, part):
    key = jax.random.fold_in(key, 7)
    base = jax.random.normal(key, (N_SECTION, D, 4 * D), jnp.float32) / math.sqrt(D)
    columns = jnp.arange(4 * D)[None, None, :]
    factor = jnp.where(columns >= 3 * D, 4.0, 1.0)
    return (base * factor).astype(jnp.bfloat16)


def draw_cross_norm(key, part):
    key = jax.random.fold_in(key, 9)
    noise = jnp.clip(jax.random.normal(key, (N_SECTION, 2, D), jnp.float32), -4.0, 4.0)
    which = jnp.arange(2)[None, :, None]
    return jnp.where(which == 0, 1.0 + 0.15 * noise, 0.3 * noise).astype(jnp.bfloat16)


def with_ends(values, key, smallest, largest):
    longest = values.shape.index(max(values.shape))
    spots = []
    for shift in (0, 1):
        where = [jax.random.randint(jax.random.fold_in(key, axis), (), 0, length) for axis, length in enumerate(values.shape)]
        where[longest] = (where[longest] + shift) % values.shape[longest]
        spots.append(tuple(where))
    return values.at[spots[0]].set(smallest).at[spots[1]].set(largest)


def strengthened(values, own_key, source, target, shards_of, factor):
    owner, partner = [(jnp.arange(values.shape[dim]) // (values.shape[dim] // shards_of)).reshape([-1 if axis == dim else 1 for axis in range(values.ndim)]) for dim in (source, target)]
    chosen = jax.random.permutation(own_key, shards_of)[partner]
    strong = (owner == chosen) | (owner == (partner + shards_of // 2) % shards_of)
    return jnp.where(strong, factor * values, values)


def levels(rng, dims, pieces, low, high):
    loudness, own = 1.0, jax.random.fold_in(rng, 6)
    for dim, shards_of in pieces:
        steps = jnp.exp(jax.random.uniform(jax.random.fold_in(own, dim), (shards_of,), jnp.float32, low / len(pieces), high / len(pieces)))
        loudness = loudness * jnp.repeat(steps, dims[dim] // shards_of).reshape([-1 if axis == dim else 1 for axis in range(len(dims))])
    return loudness


def rank_bounds(count, slope):
    loads = [(1 << 20) // math.isqrt(standing ** slope) + 1 for standing in range(1, count + 1)]
    scale = 1 + sum(loads) // (1 << 30)
    return np.cumsum(np.array([max(1, weight // scale) for weight in loads]))


def ranked(stream_key, shape, amount, slope):
    listing = rank_bounds(amount, slope)
    pick = jax.random.randint(jax.random.fold_in(stream_key, 1), shape, 0, int(listing[amount - 1]))
    standing = jnp.searchsorted(jnp.asarray(listing, jnp.int32), pick, side="right")
    return jax.random.permutation(jax.random.fold_in(stream_key, 2), amount)[standing].astype(jnp.int32)


def bell_draw(rng, dims, scale, limit, cuts=(), held_as=jnp.bfloat16):
    values = scale * jax.random.normal(rng, dims, jnp.float32)
    if cuts:
        values = values * levels(rng, dims, cuts, -0.22, 0.18)
    return jnp.clip(values, -limit, limit).astype(held_as)


def noise_with(rng, extent, scale, limit, pieces, heavy, kind=jnp.bfloat16):
    values = scale * jax.random.normal(rng, extent, jnp.float32)
    if pieces:
        values = values * levels(rng, extent, pieces, -0.22, 0.18)
    return jnp.clip(strengthened(values, jax.random.fold_in(rng, 3), *heavy), -limit, limit).astype(kind)


def setup_inputs(seed: int = 0) -> dict:
    splits = jax.random.split(jax.random.key(seed), 16)
    source = noise_with(splits[0], (PAIRS, SEQ, D), 1.0, 6.0, ((0, 8),), (0, 2, 8, 2.0))
    target = noise_with(splits[1], (PAIRS, SEQ, D), 1.0, 6.0, ((0, 8),), (0, 2, 8, 2.0))
    directions = with_ends(ranked(splits[2], (PAIRS,), NDIR, 2), jax.random.fold_in(splits[2], 3), 0, NDIR - 1).astype(jnp.int32)
    source_lengths = draw_source_lengths(jax.random.fold_in(splits[15], 71), 0)
    target_lengths = draw_target_lengths(jax.random.fold_in(splits[15], 71), 0)
    attn_in = bell_draw(splits[5], (N_SECTION, D, 3 * D), D ** -0.5, 0.1875, ((0, 4), (1, 8)))
    attn_out = bell_draw(splits[6], (N_SECTION, D, D), (D // 16) ** -0.5, 0.75, ((0, 4), (1, 8)))
    ffn_in = bell_draw(splits[7], (N_SECTION, D, FF), D ** -0.5, 0.1875, ((0, 4), (1, 8)))
    ffn_out = bell_draw(splits[8], (N_SECTION, FF, D), FF ** -0.5, 0.09375, ((0, 4), (1, 8)))
    cross_weight = draw_cross_weight(jax.random.fold_in(splits[15], 71), 0)
    norm_gain = jnp.clip(1.0 + 0.15 * jax.random.normal(splits[10], (N_SECTION, 2, D), jnp.float32), 0.25, 1.75).astype(jnp.bfloat16)
    norm_bias = bell_draw(splits[11], (N_SECTION, 2, D), 0.3, 4.0, ((0, 4),))
    cross_norm = draw_cross_norm(jax.random.fold_in(splits[15], 71), 0)
    dir_table = bell_draw(splits[13], (NDIR, D), 0.5, 6.0, (), jnp.float32)
    cotangent = bell_draw(splits[14], (PAIRS, SEQ, D), 1.0, 6.0, ((0, 8),))
    return dict(source=source, target=target, directions=directions, source_lengths=source_lengths, target_lengths=target_lengths, attn_in=attn_in, attn_out=attn_out, ffn_in=ffn_in, ffn_out=ffn_out, cross_weight=cross_weight, norm_gain=norm_gain, norm_bias=norm_bias, cross_norm=cross_norm, dir_table=dir_table, cotangent=cotangent)


@jax.custom_vjp
def low(v):
    return lax.optimization_barrier(v.astype(jnp.bfloat16)).astype(jnp.float32)

@jax.custom_vjp
def low_back(v):
    return v

def low_keep(v):
    return (low(v), None)

def low_pass(kept, grad):
    return (grad,)

def back_keep(v):
    return (v, None)

def back_low(kept, grad):
    return (low(grad),)
low.defvjp(low_keep, low_pass)
low_back.defvjp(back_keep, back_low)
encoder_alpha = 3.42
decoder_alpha = 4.16
masked_score = -1000000000.0
norm_epsilon = 1e-05
highest = lax.Precision.HIGHEST

def round_both(value):
    return low_back(low(value))

def product(operand, matrix):
    return jnp.dot(operand, matrix, precision=highest)

def layer_norm(residual, gain_vec, bias_vec):
    centre = residual - lax.optimization_barrier(jnp.mean(residual, axis=-1, keepdims=True))
    spread = lax.optimization_barrier(jnp.mean(centre * centre, axis=-1, keepdims=True))
    return centre * lax.rsqrt(spread + norm_epsilon) * gain_vec + bias_vec

def attention(query_in, key_in, query_weight, key_weight, value_weight, out_weight, allowed):
    head_width = D // HEADS

    def split_heads(tensor):
        return tensor.reshape(tensor.shape[0], tensor.shape[1], HEADS, head_width)
    queries = split_heads(round_both(product(query_in, query_weight)))
    key_rows = split_heads(round_both(product(key_in, key_weight)))
    values = split_heads(round_both(product(key_in, value_weight)))
    scores = low_back(jnp.einsum('gqhd,gkhd->ghqk', queries, key_rows, precision=highest) * (1.0 / math.sqrt(head_width)))
    attn_probs = low(jax.nn.softmax(jnp.where(allowed, scores, masked_score), axis=-1))
    mixed_heads = round_both(jnp.einsum('ghqk,gkhd->gqhd', attn_probs, values, precision=highest))
    return low_back(product(mixed_heads.reshape(query_in.shape), out_weight))

def feed_forward(hidden, in_weight, back_weight):
    pre_act = low_back(product(hidden, in_weight))
    return low_back(product(low(jax.nn.gelu(pre_act)), back_weight))

def encoder_layer(entry_rows, qkv_weight, out_weight, in_weight, back_weight, gain_rows, bias_rows, allowed):
    branch = attention(entry_rows, entry_rows, qkv_weight[:, :D], qkv_weight[:, D:2 * D], qkv_weight[:, 2 * D:], out_weight, allowed)
    hidden = layer_norm(encoder_alpha * entry_rows + branch, gain_rows[0], bias_rows[0])
    result = layer_norm(encoder_alpha * hidden + feed_forward(low(hidden), in_weight, back_weight), gain_rows[1], bias_rows[1])
    return low(result)

def decoder_layer(entry_rows, memory, qkv_weight, out_weight, in_weight, back_weight, cross_all, gain_rows, bias_rows, cross_pair, self_allowed, cross_allowed):
    branch = attention(entry_rows, entry_rows, qkv_weight[:, :D], qkv_weight[:, D:2 * D], qkv_weight[:, 2 * D:], out_weight, self_allowed)
    first_hidden = layer_norm(decoder_alpha * entry_rows + branch, gain_rows[0], bias_rows[0])
    cross_branch = attention(low(first_hidden), memory, cross_all[:, :D], cross_all[:, D:2 * D], cross_all[:, 2 * D:3 * D], cross_all[:, 3 * D:], cross_allowed)
    second_hidden = layer_norm(decoder_alpha * first_hidden + cross_branch, cross_pair[0], cross_pair[1])
    result = layer_norm(decoder_alpha * second_hidden + feed_forward(low(second_hidden), in_weight, back_weight), gain_rows[1], bias_rows[1])
    return low(result)

def stack_forward(values, source_rows, target_rows, direction_ids, source_allowed, target_allowed):
    attn_in, attn_out, ffn_in, ffn_out, cross_weight, norm_gain, norm_bias, cross_norm, dir_table, probes = values
    half_sections = N_SECTION // 2
    layer_outputs = []
    for section_pos in range(half_sections):
        entry_rows = source_rows if section_pos == 0 else layer_outputs[-1]
        entry_rows = low_back(entry_rows + probes[section_pos])
        layer_outputs.append(encoder_layer(entry_rows, attn_in[section_pos], attn_out[section_pos], ffn_in[section_pos], ffn_out[section_pos], norm_gain[section_pos], norm_bias[section_pos], source_allowed))
    memory = low_back(layer_outputs[-1])
    for layer_pos in range(half_sections):
        section_pos = half_sections + layer_pos
        if layer_pos == 0:
            entry_rows = low(target_rows + dir_table[direction_ids][:, None, :] + probes[section_pos])
        else:
            entry_rows = layer_outputs[-1] + probes[section_pos]
        entry_rows = low_back(entry_rows)
        layer_outputs.append(decoder_layer(entry_rows, memory, attn_in[section_pos], attn_out[section_pos], ffn_in[section_pos], ffn_out[section_pos], cross_weight[section_pos], norm_gain[section_pos], norm_bias[section_pos], cross_norm[section_pos], target_allowed, source_allowed))
    return jnp.stack(layer_outputs)

def reference(source, target, directions, source_lengths, target_lengths, attn_in, attn_out, ffn_in, ffn_out, cross_weight, norm_gain, norm_bias, cross_norm, dir_table, cotangent):
    params = tuple((item.astype(jnp.float32) for item in (attn_in, attn_out, ffn_in, ffn_out, cross_weight, norm_gain, norm_bias, cross_norm, dir_table)))
    positions = jnp.arange(SEQ)
    causal = positions[None, :] <= positions[:, None]

    def grouped(array):
        return array.reshape((N_DP, MICRO) + array.shape[1:])

    def group_step(totals, inputs):
        source_group, target_group, direction_group, source_len, target_len, cot_group = inputs
        source_allowed = (positions[None, :] < source_len[:, None])[:, None, None, :]
        target_allowed = (causal[None] & (positions[None, None, :] < target_len[:, None, None]))[:, None]
        probes = jnp.zeros((N_SECTION, MICRO, SEQ, D), jnp.float32)

        def forward(*values):
            return stack_forward(values, source_group.astype(jnp.float32), target_group.astype(jnp.float32), direction_group, source_allowed, target_allowed)
        stacked, pullback = jax.vjp(forward, *params + (probes,))
        seed_grads = jnp.zeros_like(stacked).at[N_SECTION - 1].set(cot_group.astype(jnp.float32))
        gradients = pullback(seed_grads)
        totals = tuple((total + grad for total, grad in zip(totals, gradients[:-1])))
        return (totals, (stacked.astype(jnp.bfloat16), gradients[-1].astype(jnp.bfloat16)))
    start_totals = tuple((jnp.zeros_like(item) for item in params))
    totals, (section_rows, section_grads) = lax.scan(group_step, start_totals, (grouped(source), grouped(target), grouped(directions), grouped(source_lengths), grouped(target_lengths), grouped(cotangent)))

    def regroup(array):
        return jnp.transpose(array, (1, 0, 2, 3, 4)).reshape(N_SECTION, N_DP * MICRO, SEQ, D)
    return (regroup(section_rows), regroup(section_grads), totals[0], totals[1], totals[2], totals[3], totals[4], totals[5], totals[6], totals[7], totals[8])
```

```python
import math
import types

import jax
import jax.numpy as jnp
from jax import lax
from jax.experimental import pallas as pl
from jax.experimental.pallas import tpu as pltpu
from jax.sharding import PartitionSpec as P

HEADS = 16
GROUP = 8
PAIR_BIT = 1
ENCODER_ALPHA = 3.42
DECODER_ALPHA = 4.16
MASKED = -1000000000.0
EPSILON = 1e-05
MESH = pl.DeviceIdType.MESH
f32, bf16 = jnp.float32, jnp.bfloat16
NN, NT, TN = (((1,), (0,)), ((), ())), (((1,), (1,)), ((), ())), (((0,), (0,)), ((), ()))
ATTN, CROSS, FFN = 0, 1, 2
QKV, FIN, FOUT, CQKV, OUT, COUT = range(6)
KIND_MATS = {ATTN: (QKV, OUT), CROSS: (CQKV, COUT), FFN: (FIN, FOUT)}
DECODER_MATS = (CQKV, COUT)


def dot(a, b, dims):
    return lax.dot_general(a, b, dims, preferred_element_type=f32)


def dv(a, b):
    return a // b if isinstance(a, int) else lax.div(a, jnp.int32(b))


def rm(a, b):
    return a % b if isinstance(a, int) else lax.rem(a, jnp.int32(b))


def mul(a, b):
    return pl.multiple_of(a * b, b)


def make_plan(sections, dp_count, pairs, seq, width, ff, directions):
    p = types.SimpleNamespace()
    p.NS, p.ND, p.L, p.half = sections, dp_count, sections, sections // 2
    p.pairs, p.seq, p.D, p.FF, p.R = pairs, seq, width, ff, pairs * seq
    p.tz = 2 if sections < GROUP and dp_count >= 4 else 1
    p.TPN = sections * p.tz
    p.K = p.TPN // 2
    p.RR = p.R // p.TPN
    p.CW = width // p.TPN
    p.HPR = HEADS // p.TPN
    p.FB = ff // p.TPN
    p.rb = width // dp_count
    p.fb = ff // dp_count // p.TPN
    p.q = dp_count // p.TPN
    p.NU = dp_count // p.tz
    p.C = p.NU // p.q
    p.cw = width // p.C
    p.NB = dp_count.bit_length() - 1
    if p.tz == 2:
        p.steps = [b for b in reversed(range(p.NB)) if b != PAIR_BIT]
    else:
        p.steps = list(range(p.NB))
    p.nst = len(p.steps)
    p.T = 2 * p.half + 3 * (p.L - p.half)
    p.NDIR = directions
    p.dir_rows = directions // sections
    p.cols = width // dp_count
    return p


def build(p):
    NS, ND, L, half, TPN, K, RR, R, D = p.NS, p.ND, p.L, p.half, p.TPN, p.K, p.RR, p.R, p.D
    CW, FB, NU, NB, nst, T, tz, q = p.CW, p.FB, p.NU, p.NB, p.nst, p.T, p.tz, p.q
    NH, LD = tz, p.L - p.half
    HB = K * RR
    C, cw = p.C, p.cw
    mat_block = {
        QKV: (p.rb, 3 * CW),
        FIN: (p.rb, FB),
        FOUT: (p.fb, D),
        CQKV: (p.rb, 3 * CW),
        OUT: (p.rb, cw),
        COUT: (p.rb, cw),
    }
    all_bits = list(reversed(range(NB)))
    mat_bits = {m: [b for b in all_bits if b in p.steps] if m in (OUT, COUT) else all_bits for m in mat_block}
    two = {m: (2,) * len(mat_bits[m]) for m in mat_block}
    back_steps = p.steps[::-1]

    vm, dma = pltpu.VMEM, pltpu.SemaphoreType.DMA
    scratch = dict(
        norms=vm((NS, 8, D), f32),
        aux=vm((NH, 8, R), f32),
        dirw=vm((NH, p.pairs, p.NDIR, 128), f32),
        cotb=vm((NH, RR, D), bf16),
        xbuf=vm((L + 2, NH, R, D), bf16),
        hb=vm((L, NH, R, D), bf16),
        h1b=vm((LD, NH, R, D), bf16),
        qkv=vm((L, NH, R, 3 * CW), bf16),
        cqkv=vm((LD, NH, R, 3 * CW), bf16),
        osv=vm((L, NH, R, CW), bf16),
        cosv=vm((LD, NH, R, CW), bf16),
        pre=vm((L, NH, R, FB), bf16),
        act=vm((R, FB), bf16),
        zs=vm((T, NH, RR, D), bf16),
        rstd=vm((T, NH, RR, 128), f32),
        res=vm((NH, RR, D), f32),
        gy=vm((NH, RR, D), f32),
        gag=vm((2, NH, R, D), bf16),
        gxo=vm((L, NH, RR, D), bf16),
        gmem=vm((NH, R, D), f32),
        gqkv=vm((NH, R, 3 * CW), bf16),
        gpre=vm((NH, R, FB), bf16),
        actb=vm((NH, R, FB), bf16),
        rsas=vm((2, NH, HB, D), bf16),
        rsar=vm((2, NH, HB, D), bf16),
        rsp=vm((NH, HB, D), f32),
        rsbs=vm((2, NH, K, RR, D), bf16),
        rsbr=vm((2, NH, K, RR, D), bf16),
        small=vm((NS, 16, D), f32),
        sm1=vm((TPN, NU * p.cols // 128, 16, 128), f32),
        sm1r=vm((TPN, NU * p.cols // 128, 16, 128), f32),
        sm2=vm((NU, 16, 128), f32),
        sm2r=vm((NU, 16, 128), f32),
        smo=vm((16, 128), f32),
        init_l=dma((5,)),
        init_s=dma((5,)),
        init_r=dma((5,)),
        norm_s=dma((NS,)),
        norm_r=dma((NS,)),
        a2a_s=dma((4, TPN)),
        a2a_r=dma((6, L, tz)),
        wo_s=dma((2, C)),
        ag_s=dma((nst, 6, L)),
        ag_r=dma((nst, 6, L)),
        tpa_s=dma((2, NH, K)),
        tpa_r=dma((2, NH, K)),
        tpf_s=dma((2, NH, K)),
        tpf_r=dma((2, NH, K)),
        rsa_s=dma((2, NH)),
        rsa_r=dma((2, NH)),
        rsb_s=dma((2, NH, K)),
        rsb_r=dma((2, NH, K)),
        gr_s=dma((nst, 6)),
        gr_r=dma((nst, 6)),
        credit=pltpu.SemaphoreType.REGULAR((nst, 3)),
        home_s=dma((6, tz)),
        home_r=dma((6, max(TPN, C))),
        sig_s=dma((L, NH)),
        sig_r=dma((TPN,)),
        sm1_s=dma((TPN,)),
        sm1_rs=dma((TPN,)),
        sm2_s=dma((NU,)),
        sm2_rs=dma((NU,)),
        out_l=dma((L,)),
        smo_l=dma((1,)),
    )
    for m, block in mat_block.items():
        scratch["w%d" % m] = vm((LD if m in DECODER_MATS else L,) + two[m] + block, bf16)
        scratch["g%d" % m] = vm(two[m] + block, bf16)
        scratch["st%d" % m] = vm((2 ** (len(two[m]) - nst),) + block, bf16)
        for j in range(1, nst + 1):
            scratch["r%d_%d" % (m, j)] = vm(two[m][j:] + block, bf16)
    in_names = ["src", "x2", "cot", "auxi", "dirwi", "normsi", "aq", "ai", "af", "ac", "woi", "wcoi"]
    out_names = ["out", "sig", "hq", "hi", "hf", "hc", "hwo", "hwco", "smout"]
    scratch_names = list(scratch)

    def kernel(*refs):
        n = types.SimpleNamespace(**dict(zip(in_names + out_names + scratch_names, refs)))
        W = {m: getattr(n, "w%d" % m) for m in mat_block}
        A = {QKV: n.aq, FIN: n.ai, FOUT: n.af, CQKV: n.ac}
        H = {QKV: n.hq, FIN: n.hi, FOUT: n.hf, CQKV: n.hc, OUT: n.hwo, COUT: n.hwco}
        G = {m: getattr(n, "g%d" % m) for m in mat_block}
        ST = {m: getattr(n, "st%d" % m) for m in mat_block}
        RB = {m: [None] + [getattr(n, "r%d_%d" % (m, j)) for j in range(1, nst + 1)] for m in mat_block}
        s, d = lax.axis_index("section"), lax.axis_index("dp")
        core, x = rm(s, 2), dv(s, 2)
        bit = [rm(dv(d, 1 << b), 2) for b in range(NB)]
        zl = bit[PAIR_BIT] if tz == 2 else 0
        k = zl * (NS // 2) + x
        r = core * K + k
        g = dv(d, 4) * 2 + rm(d, 2) if tz == 2 else d

        def place(rank, group):
            c2, k2 = dv(rank, K), rm(rank, K)
            x2, z2 = rm(k2, NS // 2), dv(k2, NS // 2)
            d2 = dv(group, 2) * 4 + z2 * 2 + rm(group, 2) if tz == 2 else group
            return (x2 * 2 + c2, d2)

        def with_bit(b, value):
            return d + (value - bit[b]) * (1 << b)

        def remote(src, dst, send, recv, device):
            return pltpu.make_async_remote_copy(
                src_ref=src, dst_ref=dst, send_sem=send, recv_sem=recv, device_id=device, device_id_type=MESH
            )

        def local(src, dst, sem):
            return pltpu.make_async_copy(src, dst, sem)

        def wait(ref, sem):
            pltpu.make_async_copy(ref, ref, sem).wait()

        sibling = place((1 - core) * K + k, g)

        barrier = pltpu.get_barrier_semaphore()
        total = NS * ND
        me = s * ND + d

        @pl.loop(1, total)
        def _(j):
            other = rm(me + j, total)
            pl.semaphore_signal(barrier, inc=1, device_id=(dv(other, ND), rm(other, ND)), device_id_type=MESH)

        pl.semaphore_wait(barrier, total - 1)

        own = pl.ds(mul(r, RR), RR)
        for j in range(1, NS):
            to = rm(s + j, NS)
            remote(n.normsi, n.norms.at[s], n.norm_s.at[j], n.norm_r.at[j], (to, d)).start()
        local(n.normsi, n.norms.at[s], n.norm_s.at[0]).start()
        other_rank = core * K + (1 - zl) * (NS // 2) + x
        other_rows = pl.ds(mul(other_rank, RR), RR)
        pair_dev = (s, with_bit(PAIR_BIT, 1 - zl)) if tz == 2 else None
        firsts = [
            (n.src, n.xbuf.at[0, zl], n.src, n.xbuf.at[0, zl]),
            (n.x2, n.xbuf.at[half + 1, zl], n.x2, n.xbuf.at[half + 1, zl]),
            (n.auxi, n.aux.at[zl], n.auxi, n.aux.at[zl]),
            (n.dirwi, n.dirw.at[zl], n.dirwi, n.dirw.at[zl]),
            (n.cot.at[own], n.cotb.at[zl], n.cot.at[other_rows], n.cotb.at[zl]),
        ]

        def first_start(i):
            a, b, c, e = firsts[i]
            local(a, b, n.init_l.at[i]).start()
            if tz == 2:
                remote(c, e, n.init_s.at[i], n.init_r.at[i], pair_dev).start()

        def first_wait(i):
            a, b, c, e = firsts[i]
            wait(b, n.init_l.at[i])
            if tz == 2:
                wait(e, n.init_s.at[i])
                wait(e, n.init_r.at[i])

        first_start(2)
        first_start(0)

        def wreg(m, l, fixed):
            idx = tuple(fixed.get(b, slice(None)) for b in mat_bits[m])
            return W[m].at[(l - half if m in DECODER_MATS else l,) + idx]

        mine = {b: bit[b] for b in range(NB)}

        def a2a_start(m):
            dst = wreg(m, s, mine)
            local(A[m].at[r], dst, n.a2a_r.at[m, s, zl]).start()
            for j in range(1, TPN):
                to = rm(r + j, TPN)
                remote(A[m].at[to], dst, n.a2a_s.at[m, j], n.a2a_r.at[m, s, zl], place(to, g)).start()

        def group_bits(m, group):
            count = len(mat_bits[m])
            return tuple(rm(dv(group, 1 << (count - 1 - i)), 2) for i in range(count))

        def out_pieces(m):
            rank = dv(d, q)
            for c in range(C):
                group = rm(d, q) * C + c
                yield c, pl.ds(c * cw, cw), group, rank, (rank == r) & (group == g)

        def out_start(m, src):
            for c, span, group, rank, here in out_pieces(m):
                dst = W[m].at[(s - half if m in DECODER_MATS else s,) + group_bits(m, group)]

                @pl.when(here)
                def _():
                    local(src.at[:, span], dst, n.a2a_r.at[m, s, 0]).start()

                @pl.when(jnp.logical_not(here))
                def _():
                    remote(src.at[:, span], dst, n.wo_s.at[m - OUT, c], n.a2a_r.at[m, s, 0], place(rank, group)).start()

        a2a_start(QKV)
        out_start(OUT, n.woi)
        a2a_start(FIN)
        a2a_start(FOUT)

        @pl.when(s >= half)
        def _():
            a2a_start(CQKV)
            out_start(COUT, n.wcoi)

        first_start(1)
        first_start(4)
        first_start(3)

        def kind_layer(t):
            td = jnp.maximum(t - 2 * half, 0)
            is_enc = t < 2 * half
            tt = jnp.maximum(t, 0)
            kind = jnp.where(is_enc, 2 * rm(tt, 2), rm(td, 3))
            layer = jnp.where(is_enc, dv(tt, 2), half + dv(td, 3))
            return kind, layer

        def groups(t, fn, after_kind=None):
            valid = (t >= 0) & (t < T)
            kind, layer = kind_layer(t)
            for kd, mats in KIND_MATS.items():

                @pl.when(valid & (kind == kd))
                def _():
                    fn(kd, mats, layer)

        def ag_region(j, m, l, flip):
            fixed = {b: bit[b] for b in p.steps[j:]}
            if flip:
                fixed[p.steps[j]] = 1 - bit[p.steps[j]]
            return wreg(m, l, fixed)

        def ag_start(j, m, l):
            reg = ag_region(j, m, l, False)
            to = (s, with_bit(p.steps[j], 1 - bit[p.steps[j]]))
            remote(reg, reg, n.ag_s.at[j, m, l], n.ag_r.at[j, m, l], to).start()

        def ag_wait(j, m, l):
            if j == 0 and m in (OUT, COUT):
                wait(wreg(m, l, mine), n.a2a_r.at[m, l, 0])
            elif j == 0:
                for z in range(tz):
                    fixed = dict(mine)
                    if tz == 2:
                        fixed[PAIR_BIT] = z
                    wait(wreg(m, l, fixed), n.a2a_r.at[m, l, z])
            else:
                wait(ag_region(j - 1, m, l, True), n.ag_r.at[j - 1, m, l])

        def advance(t):
            for j in range(1, nst + 1):

                def fn(kd, mats, l, j=j):
                    for m in mats:
                        ag_wait(j - 1, m, l)
                    for m in mats:
                        ag_start(j - 1, m, l)

                groups(t + nst + 1 - j, fn)

            def last(kd, mats, l):
                for m in mats:
                    ag_wait(nst, m, l)

            groups(t, last)

        @pl.loop(0, nst)
        def _(i):
            advance(i - nst)

        def tp_start(buf, h, st=0):
            mine_rows = buf.at[own]
            for j in range(1, K):
                k2 = rm(k + j, K)
                remote(mine_rows, mine_rows, n.tpa_s.at[st, h, j], n.tpa_r.at[st, h, j], place(core * K + k2, g)).start()
            remote(mine_rows, mine_rows, n.tpa_s.at[st, h, 0], n.tpa_r.at[st, h, 0], sibling).start()

        def tp_finish(buf, h, st=0):
            def rows(c2, k2):
                return buf.at[pl.ds(mul(c2 * K + k2, RR), RR)]

            for j in range(1, K):
                k2 = rm(k - j + K, K)
                ref = rows(core, k2)
                wait(ref, n.tpa_r.at[st, h, j])
                remote(ref, ref, n.tpf_s.at[st, h, j], n.tpf_r.at[st, h, j], sibling).start()
            wait(rows(1 - core, k), n.tpa_r.at[st, h, 0])
            for j in range(1, K):
                wait(rows(1 - core, rm(k - j + K, K)), n.tpf_r.at[st, h, j])
            for j in range(K):
                wait(rows(core, k), n.tpa_s.at[st, h, j])
            for j in range(1, K):
                wait(rows(core, rm(k - j + K, K)), n.tpf_s.at[st, h, j])

        def rs_start(st, h, partial):
            n.rsas[st, h] = partial(mul(1 - core, HB)).astype(bf16)
            copy = remote(n.rsas.at[st, h], n.rsar.at[st, h], n.rsa_s.at[st, h], n.rsa_r.at[st, h], sibling)
            copy.start()
            n.rsp[h] = partial(mul(core, HB))
            wait(n.rsar.at[st, h], n.rsa_r.at[st, h])
            for j in range(1, K):
                k2 = rm(k + j, K)
                rows = pl.ds(mul(k2, RR), RR)
                n.rsbs[st, h, j] = (n.rsp[h, rows] + n.rsar[st, h, rows].astype(f32)).astype(bf16)
                remote(
                    n.rsbs.at[st, h, j],
                    n.rsbr.at[st, h, j],
                    n.rsb_s.at[st, h, j],
                    n.rsb_r.at[st, h, j],
                    place(core * K + k2, g),
                ).start()
            rows = pl.ds(mul(k, RR), RR)
            n.rsp[h, rows] = n.rsp[h, rows] + n.rsar[st, h, rows].astype(f32)
            wait(n.rsas.at[st, h], n.rsa_s.at[st, h])

        def rs_finish(st, h):
            acc = n.rsp[h, pl.ds(mul(k, RR), RR)]
            for j in range(1, K):
                wait(n.rsbr.at[st, h, j], n.rsb_r.at[st, h, j])
                acc = acc + n.rsbr[st, h, j].astype(f32)
            for j in range(1, K):
                wait(n.rsbs.at[st, h, j], n.rsb_s.at[st, h, j])
            return acc

        def halves(fn):
            if NH == 1:
                fn(0)
            else:
                pl.loop(0, NH)(fn)

        def weight(m, l, lo=0, hi=None):
            hi = mat_block[m][1] if hi is None else hi
            at = (l - half if m in DECODER_MATS else l,) + (slice(None),) * (NB + 1) + (slice(lo, hi),)
            return W[m][at].reshape((-1, hi - lo))

        def out_weight(m, l, c):
            parts = [W[m][(l - half if m in DECODER_MATS else l,) + group_bits(m, a * C + c)] for a in range(q)]
            return parts[0] if q == 1 else jnp.concatenate(parts, axis=0)

        def out_product(rows, m, l):
            return jnp.concatenate([dot(rows, out_weight(m, l, c), NN) for c in range(C)], axis=1)

        def out_product_back(grad, m, l):
            acc = None
            for c in range(C):
                term = dot(grad[:, c * cw : (c + 1) * cw], out_weight(m, l, c), NT)
                acc = term if acc is None else acc + term
            return acc

        def norm_row(l, row):
            return n.norms[l][row : row + 1, :]

        def ln_forward(t, h, value, gain, bias):
            centre = value - jnp.mean(value, axis=-1, keepdims=True)
            scale = lax.rsqrt(jnp.mean(centre * centre, axis=-1, keepdims=True) + EPSILON)
            z = centre * scale
            n.zs[t, h] = z.astype(bf16)
            n.rstd[t, h] = jnp.broadcast_to(scale, (RR, 128))
            return z * gain + bias

        def ln_backward(t, h, grad, l, gain_row, bias_row):
            z = n.zs[t, h].astype(f32)
            scale = n.rstd[t, h][:, :1]
            n.small[l, gain_row : gain_row + 1, :] += jnp.sum(grad * z, axis=0, keepdims=True)
            n.small[l, bias_row : bias_row + 1, :] += jnp.sum(grad, axis=0, keepdims=True)
            gz = grad * norm_row(l, gain_row)
            return scale * (
                gz - jnp.mean(gz, axis=-1, keepdims=True) - z * jnp.mean(gz * z, axis=-1, keepdims=True)
            )

        head_width = D // HEADS
        score_scale = 1.0 / math.sqrt(head_width)

        def allowed_of(h, causal):
            rows = lax.broadcasted_iota(jnp.int32, (R, R), 0)
            cols = lax.broadcasted_iota(jnp.int32, (R, R), 1)
            ok = (dv_vec(rows) == dv_vec(cols)) & (n.aux[h][1:2] > 0.5 if causal else n.aux[h][0:1] > 0.5)
            return ok & (cols <= rows) if causal else ok

        def dv_vec(v):
            return lax.div(v, jnp.full_like(v, p.seq))

        def head_lanes(head):
            lane = lax.broadcasted_iota(jnp.int32, (1, CW), 1)
            return (lane >= head * head_width) & (lane < (head + 1) * head_width)

        def only(value, head):
            return jnp.where(head_lanes(head), value, jnp.zeros_like(value))

        def probabilities(qs, ks, allowed, head):
            scores = dot(only(qs, head), ks, NT) * score_scale
            scores = jnp.where(allowed, scores, MASKED)
            e = jnp.exp(scores - jnp.max(scores, axis=-1, keepdims=True))
            return e / jnp.sum(e, axis=-1, keepdims=True)

        def attend(qs, ks, vs, allowed):
            out = jnp.zeros((R, CW), f32)
            for head in range(p.HPR):
                probs = probabilities(qs, ks, allowed, head)
                out = out + only(dot(probs.astype(bf16), vs, NN), head)
            return out.astype(bf16)

        def attend_back(qs, ks, vs, allowed, grad):
            gq = gk = gv = jnp.zeros((R, CW), f32)
            for head in range(p.HPR):
                probs = probabilities(qs, ks, allowed, head)
                gp = dot(only(grad, head), vs, NT)
                gs = (probs * (gp - jnp.sum(gp * probs, axis=-1, keepdims=True))).astype(bf16)
                gv = gv + only(dot(probs.astype(bf16), grad, TN), head)
                gq = gq + only(dot(gs, ks, NN), head)
                gk = gk + only(dot(gs, qs, TN), head)
            return (gq * score_scale).astype(bf16), (gk * score_scale).astype(bf16), gv.astype(bf16)

        def split3(value):
            return value[:, :CW], value[:, CW : 2 * CW], value[:, 2 * CW :]

        c0, c1 = math.sqrt(2.0 / math.pi), 0.044715

        def gelu(v):
            return 0.5 * v * (1.0 + jnp.tanh(c0 * (v + c1 * (v * v * v))))

        def gelu_slope(v):
            th = jnp.tanh(c0 * (v + c1 * (v * v * v)))
            return 0.5 * (1.0 + th) + 0.5 * v * (1.0 - th * th) * (c0 * (1.0 + 3.0 * c1 * v * v))

        def self_forward(l, t, xi, causal, alpha, into):
            advance(t)

            def first(h):
                n.qkv[l, h] = dot(n.xbuf[xi, h], weight(QKV, l), NN).astype(bf16)
                qs, ks, vs = split3(n.qkv[l, h])
                n.osv[l, h] = attend(qs, ks, vs, allowed_of(h, causal))
                rs_start(0, h, lambda row: out_product(n.osv[l, h, pl.ds(row, HB)], OUT, l))

            def second(h):
                value = alpha * n.xbuf[xi, h, own].astype(f32) + rs_finish(0, h)
                hidden = ln_forward(t, h, value, norm_row(l, 0), norm_row(l, 2))
                n.res[h] = hidden
                into[h, own] = hidden.astype(bf16)
                tp_start(into.at[h], h)

            halves(first)
            halves(second)

        def cross_forward(l, t):
            advance(t)
            ld = l - half

            def first(h):
                n.cqkv[ld, h, :, CW:] = dot(n.xbuf[half, h], weight(CQKV, l, CW), NN).astype(bf16)
                tp_finish(n.h1b.at[ld, h], h)
                n.cqkv[ld, h, :, :CW] = dot(n.h1b[ld, h], weight(CQKV, l, 0, CW), NN).astype(bf16)
                qs, ks, vs = split3(n.cqkv[ld, h])
                n.cosv[ld, h] = attend(qs, ks, vs, allowed_of(h, False))
                rs_start(0, h, lambda row: out_product(n.cosv[ld, h, pl.ds(row, HB)], COUT, l))

            def second(h):
                value = DECODER_ALPHA * n.res[h] + rs_finish(0, h)
                hidden = ln_forward(t, h, value, norm_row(l, 4), norm_row(l, 5))
                n.res[h] = hidden
                n.hb[l, h, own] = hidden.astype(bf16)
                tp_start(n.hb.at[l, h], h)

            halves(first)
            halves(second)

        def ffn_forward(l, t, xo, alpha):
            advance(t)

            def first(h):
                tp_finish(n.hb.at[l, h], h)
                before = dot(n.hb[l, h], weight(FIN, l), NN)
                n.pre[l, h] = before.astype(bf16)
                n.act[...] = gelu(before).astype(bf16)
                rs_start(0, h, lambda row: dot(n.act[pl.ds(row, HB)], weight(FOUT, l), NN))

            def second(h):
                value = alpha * n.res[h] + rs_finish(0, h)
                result = ln_forward(t, h, value, norm_row(l, 1), norm_row(l, 3))
                n.xbuf[xo, h, own] = result.astype(bf16)
                tp_start(n.xbuf.at[xo, h], h, 1)

            def third(h):
                tp_finish(n.xbuf.at[xo, h], h, 1)

            halves(first)
            halves(second)
            halves(third)

            @pl.when(s == l)
            def _():
                local(n.xbuf.at[xo, zl], n.out, n.out_l.at[0]).start()

        for i in (2, 0):
            first_wait(i)
        for j in range(1, NS):
            wait(n.norms.at[rm(s - j + NS, NS)], n.norm_r.at[j])
        wait(n.norms.at[s], n.norm_s.at[0])
        n.small[...] = jnp.zeros_like(n.small)
        n.gmem[...] = jnp.zeros_like(n.gmem)

        @pl.loop(0, half)
        def _(l):
            self_forward(l, 2 * l, l, False, ENCODER_ALPHA, n.hb.at[l])
            ffn_forward(l, 2 * l + 1, l + 1, ENCODER_ALPHA)

        for i in (1, 3, 4):
            first_wait(i)

        @pl.loop(half, L)
        def _(l):
            t = 2 * half + 3 * (l - half)
            self_forward(l, t, l + 1, True, DECODER_ALPHA, n.h1b.at[l - half])
            cross_forward(l, t + 1)
            ffn_forward(l, t + 2, l + 2, DECODER_ALPHA)

        def gregion(m, fixed):
            return G[m].at[tuple(fixed.get(b, slice(None)) for b in mat_bits[m])]

        def partner(j):
            b = back_steps[j - 1]
            return (s, with_bit(b, 1 - bit[b]))

        def gr_start(j, kd, mats, l):
            @pl.when(l != L - 1)
            def _():
                pl.semaphore_wait(n.credit.at[j - 1, kd], 1)

            for m in mats:
                fixed = {b: bit[b] for b in back_steps[: j - 1]}
                fixed[back_steps[j - 1]] = 1 - bit[back_steps[j - 1]]
                remote(
                    gregion(m, fixed), RB[m][j], n.gr_s.at[j - 1, m], n.gr_r.at[j - 1, m], partner(j)
                ).start()

        def blocks_of(count):
            return [
                tuple((i >> b) & 1 for b in reversed(range(count))) for i in range(1 << count)
            ]

        def gr_finish(j, kd, mats, l):
            for m in mats:
                wait(RB[m][j], n.gr_r.at[j - 1, m])
                mine_part = gregion(m, {b: bit[b] for b in back_steps[:j]})
                for idx in blocks_of(len(mat_bits[m]) - j):
                    value = mine_part[idx].astype(f32) + RB[m][j][idx].astype(f32)
                    if j == nst:
                        ST[m][idx if idx else 0] = value.astype(bf16)
                    else:
                        mine_part[idx] = value.astype(bf16)
                wait(RB[m][j], n.gr_s.at[j - 1, m])

            @pl.when(l != (half if kd == CROSS else 0))
            def _():
                pl.semaphore_signal(n.credit.at[j - 1, kd], inc=1, device_id=partner(j), device_id_type=MESH)

        def home(m, l, z, act):
            src = ST[m].at[z]
            if m in (OUT, COUT):
                piece = rm(g, C)
                to = (l, r * q + dv(g, C))
                here = (l == s) & (to[1] == d)
                dst, slot = H[m].at[:, pl.ds(mul(piece, cw), cw)], piece
            else:
                to = (l, with_bit(PAIR_BIT, z) if tz == 2 else d)
                here = (l == s) & (zl == z) if tz == 2 else l == s
                dst, slot = H[m].at[r], r

            if act == "wait":
                wait(src, n.home_s.at[m, z])
                return

            @pl.when(here)
            def _():
                local(src, dst, n.home_s.at[m, z]).start()

            @pl.when(jnp.logical_not(here))
            def _():
                remote(src, dst, n.home_s.at[m, z], n.home_r.at[m, slot], to).start()

        def process(u):
            def old(kd, mats, l):
                for m in mats:
                    for z in range(ST[m].shape[0]):
                        home(m, l, z, "wait")

            groups(T - 1 - (u - nst - 1), old)
            for j in range(nst, 0, -1):

                def fn(kd, mats, l, j=j):
                    gr_finish(j, kd, mats, l)
                    if j < nst:
                        gr_start(j + 1, kd, mats, l)
                    else:
                        for m in mats:
                            for z in range(ST[m].shape[0]):
                                home(m, l, z, "start")

                groups(T - 1 - (u - j), fn)

        def weight_grad(m, lefts, rights):
            rows, cols = mat_block[m]
            count = max(1, 128 // rows)
            tile = rows * count

            @pl.loop(0, ND // count)
            def _(i):
                span = pl.ds(mul(i, tile), tile)
                parts = []
                for left, right in zip(lefts, rights):
                    acc = None
                    for h in range(NH):
                        term = dot(left[h][:, span], right[h][...], TN)
                        acc = term if acc is None else acc + term
                    parts.append(acc)
                value = parts[0] if len(parts) == 1 else jnp.concatenate(parts, axis=1)
                value = value.astype(bf16)
                for e in range(count):
                    at = i * count + e
                    idx = tuple(rm(dv(at, 1 << b), 2) for b in reversed(range(NB)))
                    G[m][idx] = value[e * rows : (e + 1) * rows]

        def out_grad(m, left, right):
            for c in range(C):
                acc = None
                for h in range(NH):
                    term = dot(left[h][...], right[h][:, c * cw : (c + 1) * cw], TN)
                    acc = term if acc is None else acc + term
                acc = acc.astype(bf16)
                for a in range(q):
                    G[m][group_bits(m, a * C + c)] = acc[a * p.rb : (a + 1) * p.rb]

        def each(ref):
            return [ref.at[h] for h in range(NH)]

        def branch_grad(t, l, u, gain_row, bias_row):
            gag = n.gag.at[rm(u, 2)]

            def fn(h):
                grad = ln_backward(t, h, n.gy[h], l, gain_row, bias_row)
                n.res[h] = grad
                gag[h, own] = grad.astype(bf16)
                tp_start(gag.at[h], h)

            halves(fn)
            return gag

        def ffn_backward(l, t, u, alpha):
            gag = branch_grad(t, l, u, 1, 3)

            def first(h):
                tp_finish(gag.at[h], h)
                before = n.pre[l, h].astype(f32)
                gact = dot(gag[h], weight(FOUT, l), NT)
                n.gpre[h] = (gact * gelu_slope(before)).astype(bf16)
                rs_start(0, h, lambda row: dot(n.gpre[h, pl.ds(row, HB)], weight(FIN, l), NT))
                n.actb[h] = gelu(before).astype(bf16)

            halves(first)
            process(u)
            weight_grad(FOUT, [each(n.actb)], [each(gag)])
            weight_grad(FIN, [each(n.hb.at[l])], [each(n.gpre)])
            gr_start(1, FFN, KIND_MATS[FFN], l)

            def second(h):
                n.gy[h] = alpha * n.res[h] + rs_finish(0, h)

            halves(second)

        def cross_backward(l, t, u):
            gag = branch_grad(t, l, u, 4, 5)
            ld = l - half

            def first(h):
                tp_finish(gag.at[h], h)
                grad = out_product_back(gag.at[h], COUT, l).astype(bf16)
                qs, ks, vs = split3(n.cqkv[ld, h])
                gq, gk, gv = attend_back(qs, ks, vs, allowed_of(h, False), grad)
                n.gqkv[h, :, :CW] = gq
                n.gqkv[h, :, CW : 2 * CW] = gk
                n.gqkv[h, :, 2 * CW :] = gv
                rs_start(
                    0, h, lambda row: dot(n.gqkv[h, pl.ds(row, HB), :CW], weight(CQKV, l, 0, CW), NT)
                )
                n.gmem[h] += dot(n.gqkv[h, :, CW:], weight(CQKV, l, CW), NT)

            halves(first)
            process(u)
            out_grad(COUT, each(n.cosv.at[ld]), each(gag))
            weight_grad(
                CQKV,
                [each(n.h1b.at[ld]), each(n.xbuf.at[half])],
                [
                    [n.gqkv.at[h, :, pl.ds(0, CW)] for h in range(NH)],
                    [n.gqkv.at[h, :, pl.ds(CW, 2 * CW)] for h in range(NH)],
                ],
            )
            gr_start(1, CROSS, KIND_MATS[CROSS], l)

            def second(h):
                n.gy[h] = DECODER_ALPHA * n.res[h] + rs_finish(0, h)

            halves(second)

        def sig_copy(l, h, act):
            here = (l == s) & (h == zl)
            src = n.gxo.at[l, h]

            @pl.when(here)
            def _():
                if act == "start":
                    local(src, n.sig.at[own], n.sig_r.at[r]).start()

            @pl.when(jnp.logical_not(here))
            def _():
                if act == "start":
                    to = (l, with_bit(PAIR_BIT, h) if tz == 2 else d)
                    remote(src, n.sig.at[own], n.sig_s.at[l, h], n.sig_r.at[r], to).start()
                else:
                    wait(src, n.sig_s.at[l, h])

        def self_backward(l, t, u, xi, causal, alpha):
            gag = branch_grad(t, l, u, 0, 2)

            def first(h):
                tp_finish(gag.at[h], h)
                grad = out_product_back(gag.at[h], OUT, l).astype(bf16)
                qs, ks, vs = split3(n.qkv[l, h])
                gq, gk, gv = attend_back(qs, ks, vs, allowed_of(h, causal), grad)
                n.gqkv[h, :, :CW] = gq
                n.gqkv[h, :, CW : 2 * CW] = gk
                n.gqkv[h, :, 2 * CW :] = gv
                rs_start(0, h, lambda row: dot(n.gqkv[h, pl.ds(row, HB)], weight(QKV, l), NT))

            halves(first)
            process(u)
            out_grad(OUT, each(n.osv.at[l]), each(gag))
            weight_grad(QKV, [each(n.xbuf.at[xi])], [each(n.gqkv)])
            gr_start(1, ATTN, KIND_MATS[ATTN], l)

            def second(h):
                grad = (alpha * n.res[h] + rs_finish(0, h)).astype(bf16)
                n.gxo[l, h] = grad
                n.gy[h] = grad.astype(f32)
                sig_copy(l, h, "start")

            halves(second)

        def seed(h):
            n.gy[h] = n.cotb[h].astype(f32)

        halves(seed)

        @pl.loop(0, LD)
        def _(i):
            l = L - 1 - i
            t = 2 * half + 3 * (l - half)
            ffn_backward(l, t + 2, 3 * i, DECODER_ALPHA)
            cross_backward(l, t + 1, 3 * i + 1)
            self_backward(l, t, 3 * i + 2, l + 1, True, DECODER_ALPHA)

        def directions(h):
            column = n.dirw[h, dv(r * RR, p.seq)][:, :1]
            rows = column * jnp.sum(n.gy[h], axis=0, keepdims=True)
            for sec in range(NS):
                lo = sec * p.dir_rows
                n.small[sec, 8 : 8 + p.dir_rows, :] += rows[lo : lo + p.dir_rows]

        halves(directions)

        def memory_first(h):
            rs_start(1, h, lambda row: n.gmem[h, pl.ds(row, HB)])

        def memory_second(h):
            n.gy[h] = rs_finish(1, h).astype(bf16).astype(f32)

        halves(memory_first)
        halves(memory_second)

        @pl.loop(0, half)
        def _(i):
            l = half - 1 - i
            u = 3 * LD + 2 * i
            ffn_backward(l, 2 * l + 1, u, ENCODER_ALPHA)
            self_backward(l, 2 * l, u + 1, l, False, ENCODER_ALPHA)

        for rank in range(TPN):
            for g2 in range(NU):
                sec, d2 = place(rank, g2)
                lo = d2 * p.cols
                tile, lane = divmod(g2 * p.cols, 128)
                n.sm1[rank, tile, :, lane : lane + p.cols] = n.small[sec, :, lo : lo + p.cols]
        for j in range(1, TPN):
            to = rm(r + j, TPN)
            remote(n.sm1.at[to], n.sm1r.at[j], n.sm1_s.at[j], n.sm1_rs.at[j], place(to, g)).start()

        @pl.loop(0, nst + 1)
        def _(i):
            process(T + i)

        total_small = n.sm1[r]
        for j in range(1, TPN):
            wait(n.sm1r.at[j], n.sm1_rs.at[j])
            total_small = total_small + n.sm1r[j]
        for g2 in range(NU):
            tile, lane = divmod(g2 * p.cols, 128)
            n.sm2[g2, :, : p.cols] = total_small[tile, :, lane : lane + p.cols]
        for j in range(1, NU):
            to = rm(g + j, NU)
            remote(n.sm2.at[to], n.sm2r.at[j], n.sm2_s.at[j], n.sm2_rs.at[j], place(r, to)).start()
        mine_small = n.sm2[g]
        for j in range(1, NU):
            wait(n.sm2r.at[j], n.sm2_rs.at[j])
            mine_small = mine_small + n.sm2r[j]
        n.smo[...] = mine_small
        local(n.smo, n.smout, n.smo_l.at[0]).start()
        wait(n.smo, n.smo_l.at[0])

        def home_wait(m):
            for j in range(1, TPN):
                rank = rm(r + j, TPN)
                wait(H[m].at[rank], n.home_r.at[m, rank])

        def home_wait_out(m):
            for c, span, group, rank, here in out_pieces(m):

                @pl.when(jnp.logical_not(here))
                def _():
                    wait(H[m].at[:, span], n.home_r.at[m, c])

        for m in (QKV, FIN, FOUT):
            home_wait(m)
        home_wait_out(OUT)

        @pl.when(s >= half)
        def _():
            home_wait(CQKV)
            home_wait_out(COUT)

        for rank in range(TPN):
            wait(n.sig.at[pl.ds(rank * RR, RR)], n.sig_r.at[rank])
        wait(n.out, n.out_l.at[0])
        for l in range(L):
            for h in range(NH):
                sig_copy(l, h, "wait")
        for j in range(1, TPN):
            wait(n.sm1.at[0], n.sm1_s.at[j])
        for j in range(1, NU):
            wait(n.sm2.at[0], n.sm2_s.at[j])
        for j in range(1, NS):
            wait(n.norms.at[0], n.norm_s.at[j])
        for j in range(1, TPN):
            for m in (QKV, FIN, FOUT):
                wait(A[m].at[0], n.a2a_s.at[m, j])

        @pl.when(s >= half)
        def _():
            for j in range(1, TPN):
                wait(A[CQKV].at[0], n.a2a_s.at[CQKV, j])

        for m in (OUT, COUT):
            for c, span, group, rank, here in out_pieces(m):
                sends = jnp.logical_not(here) if m == OUT else jnp.logical_not(here) & (s >= half)

                @pl.when(sends)
                def _():
                    wait(n.woi.at[:, span], n.wo_s.at[m - OUT, c])

        @pl.loop(0, L)
        def _(l):
            for j in range(nst):
                for m in mat_block:
                    if m not in DECODER_MATS:
                        wait(ag_region(j, m, l, False), n.ag_s.at[j, m, l])

                @pl.when(l >= half)
                def _():
                    for m in DECODER_MATS:
                        wait(ag_region(j, m, l, False), n.ag_s.at[j, m, l])

    def sd(*shape, dtype=bf16):
        return jax.ShapeDtypeStruct(shape, dtype)

    def blocks(m, lead):
        return sd(lead, *mat_block[m])

    outs = [
        sd(R, D),
        sd(R, D),
        blocks(QKV, TPN),
        blocks(FIN, TPN),
        blocks(FOUT, TPN),
        blocks(CQKV, TPN),
        sd(p.rb, D),
        sd(p.rb, D),
        sd(16, 128, dtype=f32),
    ]
    anywhere = pl.BlockSpec(memory_space=pl.ANY)
    return pl.pallas_call(
        kernel,
        out_shape=outs,
        in_specs=[anywhere] * len(in_names),
        out_specs=[anywhere] * len(out_names),
        scratch_shapes=list(scratch.values()),
        compiler_params=pltpu.CompilerParams(
            collective_id=0, has_side_effects=True, vmem_limit_bytes=64 * 1024 * 1024 - 64 * 1024
        ),
    )


def solution(mesh):
    def body(
        source,
        target,
        directions,
        source_lengths,
        target_lengths,
        attn_in,
        attn_out,
        ffn_in,
        ffn_out,
        cross_weight,
        norm_gain,
        norm_bias,
        cross_norm,
        dir_table,
        cotangent,
    ):
        pairs, seq, width = source.shape
        p = make_plan(
            mesh.shape["section"], mesh.shape["dp"], pairs, seq, width, ffn_in.shape[2], dir_table.shape[0]
        )
        section = lax.axis_index("section")
        routing = (directions[:, None] == jnp.arange(p.NDIR)[None, :]).astype(f32)
        rows = jnp.dot(routing, dir_table, precision=lax.Precision.HIGHEST)
        x2 = (target.astype(f32) + rows[:, None, :]).astype(bf16).reshape(p.R, width)
        positions = jnp.arange(seq)
        valid = [(positions[None, :] < lens[:, None]).astype(f32).reshape(1, p.R) for lens in (source_lengths, target_lengths)]
        aux = jnp.concatenate(valid + [jnp.zeros((6, p.R), f32)], axis=0)
        dirw = jnp.broadcast_to(routing[:, :, None], (pairs, p.NDIR, 128))
        norms = jnp.concatenate(
            (norm_gain[0], norm_bias[0], cross_norm[0], jnp.zeros((2, width), bf16)), axis=0
        ).astype(f32)
        aq = attn_in[0].reshape(p.rb, 3, p.TPN, p.CW).transpose(2, 0, 1, 3).reshape(p.TPN, p.rb, 3 * p.CW)
        cross = cross_weight[0][:, : 3 * width]
        ac = cross.reshape(p.rb, 3, p.TPN, p.CW).transpose(2, 0, 1, 3).reshape(p.TPN, p.rb, 3 * p.CW)
        ai = ffn_in[0].reshape(p.rb, p.ND, p.TPN, p.fb).transpose(2, 0, 1, 3).reshape(p.TPN, p.rb, p.FB)
        af = ffn_out[0].reshape(p.TPN, p.fb, width)
        out, sig, hq, hi, hf, hc, hwo, hwco, small = build(p)(
            source.reshape(p.R, width),
            x2,
            cotangent.reshape(p.R, width),
            aux,
            dirw,
            norms,
            aq,
            ai,
            af,
            ac,
            attn_out[0],
            cross_weight[0][:, 3 * width :],
        )
        decoder = section >= p.half

        def heads_back(value):
            value = value.reshape(p.TPN, p.rb, 3, p.CW).transpose(1, 2, 0, 3)
            return value.reshape(1, p.rb, 3 * width).astype(f32)

        g_in = hi.reshape(p.TPN, p.rb, p.ND, p.fb).transpose(1, 2, 0, 3).reshape(1, p.rb, p.FF).astype(f32)
        g_out = hf.reshape(1, p.TPN * p.fb, width).astype(f32)
        g_wo = hwo.astype(f32)[None]
        g_cross = jnp.concatenate((heads_back(hc), hwco.astype(f32)[None]), axis=2)
        g_cross = jnp.where(decoder, g_cross, jnp.zeros_like(g_cross))
        small = small[:, : p.cols]
        return (
            out.reshape(1, pairs, seq, width),
            sig.reshape(1, pairs, seq, width),
            heads_back(hq),
            g_wo,
            g_in,
            g_out,
            g_cross,
            small[None, 0:2],
            small[None, 2:4],
            small[None, 4:6],
            small[8 : 8 + p.dir_rows],
        )

    sharded = P("section", "dp", None)
    return jax.shard_map(
        body,
        mesh=mesh,
        in_specs=(
            P("dp", None, None),
            P("dp", None, None),
            P("dp"),
            P("dp"),
            P("dp"),
            sharded,
            sharded,
            sharded,
            sharded,
            sharded,
            P("section", None, None),
            P("section", None, None),
            P("section", None, None),
            P(),
            P("dp", None, None),
        ),
        out_specs=(
            P("section", "dp", None, None),
            P("section", "dp", None, None),
            sharded,
            sharded,
            sharded,
            sharded,
            sharded,
            P("section", None, "dp"),
            P("section", None, "dp"),
            P("section", None, "dp"),
            P("section", "dp"),
        ),
        check_vma=False,
    )
```

```python
import math
import types

import jax
import jax.numpy as jnp
from jax import lax
from jax.experimental import pallas as pl
from jax.experimental.pallas import tpu as pltpu
from jax.sharding import PartitionSpec as P

HEADS = 16
GROUP = 8
AHEAD = (4, 3, 2)
BEHIND = (2, 3)
PAIR_BIT = 0
ENCODER_ALPHA = 3.42
DECODER_ALPHA = 4.16
MASKED = -1000000000.0
EPSILON = 1e-05
MESH = pl.DeviceIdType.MESH
f32, bf16 = jnp.float32, jnp.bfloat16
NN, NT, TN = (((1,), (0,)), ((), ())), (((1,), (1,)), ((), ())), (((0,), (0,)), ((), ()))
ATTN, CROSS, FFN = 0, 1, 2
QKV, FIN, FOUT, CQKV, OUT, COUT = range(6)
KIND_MATS = {ATTN: (QKV, OUT), CROSS: (CQKV, COUT), FFN: (FIN, FOUT)}
DECODER_MATS = (CQKV, COUT)


def dot(a, b, dims):
    return lax.dot_general(a, b, dims, preferred_element_type=f32)


def dv(a, b):
    return a // b if isinstance(a, int) else lax.div(a, jnp.int32(b))


def rm(a, b):
    return a % b if isinstance(a, int) else lax.rem(a, jnp.int32(b))


def mul(a, b):
    return pl.multiple_of(a * b, b)


def make_plan(sections, dp_count, pairs, seq, width, ff, directions):
    p = types.SimpleNamespace()
    p.NS, p.ND, p.L, p.half = sections, dp_count, sections, sections // 2
    p.pairs, p.seq, p.D, p.FF, p.R = pairs, seq, width, ff, pairs * seq
    p.tz = 2 if sections < GROUP and dp_count >= 4 else 1
    p.TPN = sections * p.tz
    p.K = p.TPN // 2
    p.RR = p.R // p.TPN
    p.CW = width // p.TPN
    p.HPR = HEADS // p.TPN
    p.FB = ff // p.TPN
    p.rb = width // dp_count
    p.fb = ff // dp_count // p.TPN
    p.q = dp_count // p.TPN
    p.NU = dp_count // p.tz
    p.C = p.NU // p.q
    p.cw = width // p.C
    p.NB = dp_count.bit_length() - 1
    if p.tz == 2:
        p.steps = [b for b in reversed(range(p.NB)) if b != PAIR_BIT]
    else:
        p.steps = list(range(p.NB))
    p.nst = len(p.steps)
    p.T = 2 * p.half + 3 * (p.L - p.half)
    p.NDIR = directions
    p.dir_rows = directions // sections
    p.cols = width // dp_count
    return p


def build(p):
    NS, ND, L, half, TPN, K, RR, R, D = p.NS, p.ND, p.L, p.half, p.TPN, p.K, p.RR, p.R, p.D
    CW, FB, NU, NB, nst, T, tz, q = p.CW, p.FB, p.NU, p.NB, p.nst, p.T, p.tz, p.q
    NH, LD = tz, p.L - p.half
    HB = K * RR
    C, cw = p.C, p.cw
    mat_block = {
        QKV: (p.rb, 3 * CW),
        FIN: (p.rb, FB),
        FOUT: (p.fb, D),
        CQKV: (p.rb, 3 * CW),
        OUT: (p.rb, cw),
        COUT: (p.rb, cw),
    }
    all_bits = list(reversed(range(NB)))
    mat_bits = {m: [b for b in all_bits if b in p.steps] if m in (OUT, COUT) else all_bits for m in mat_block}
    two = {m: (2,) * len(mat_bits[m]) for m in mat_block}
    back_steps = p.steps[::-1]

    vm, dma = pltpu.VMEM, pltpu.SemaphoreType.DMA
    scratch = dict(
        norms=vm((NS, 8, D), f32),
        aux=vm((NH, 8, R), f32),
        dirw=vm((NH, p.pairs, p.NDIR, 128), f32),
        cotb=vm((NH, RR, D), bf16),
        xbuf=vm((L + 2, NH, R, D), bf16),
        hb=vm((L, NH, R, D), bf16),
        h1b=vm((LD, NH, R, D), bf16),
        qkv=vm((L, NH, R, 3 * CW), bf16),
        cqkv=vm((LD, NH, R, 3 * CW), bf16),
        osv=vm((L, NH, R, CW), bf16),
        cosv=vm((LD, NH, R, CW), bf16),
        pre=vm((L, NH, R, FB), bf16),
        act=vm((R, FB), bf16),
        zs=vm((T, NH, RR, D), bf16),
        rstd=vm((T, NH, RR, 128), f32),
        res=vm((NH, RR, D), f32),
        gy=vm((NH, RR, D), f32),
        gag=vm((2, NH, R, D), bf16),
        gxo=vm((L, NH, RR, D), bf16),
        gmem=vm((NH, R, D), f32),
        gqkv=vm((NH, R, 3 * CW), bf16),
        gpre=vm((NH, R, FB), bf16),
        actb=vm((NH, R, FB), bf16),
        rsas=vm((2, NH, HB, D), bf16),
        rsar=vm((2, NH, HB, D), bf16),
        rsp=vm((NH, HB, D), f32),
        rsbs=vm((2, NH, K, RR, D), bf16),
        rsbr=vm((2, NH, K, RR, D), bf16),
        small=vm((NS, 16, D), f32),
        sm1=vm((TPN, NU * p.cols // 128, 16, 128), f32),
        sm1r=vm((TPN, NU * p.cols // 128, 16, 128), f32),
        sm2=vm((NU, 16, 128), f32),
        sm2r=vm((NU, 16, 128), f32),
        smo=vm((16, 128), f32),
        init_l=dma((5,)),
        init_s=dma((5,)),
        init_r=dma((5,)),
        norm_s=dma((NS,)),
        norm_r=dma((NS,)),
        a2a_s=dma((4, TPN)),
        a2a_r=dma((6, L, tz)),
        wo_s=dma((2, C)),
        ag_s=dma((nst, 6, L)),
        ag_r=dma((nst, 6, L)),
        tpa_s=dma((2, NH, K)),
        tpa_r=dma((2, NH, K)),
        tpf_s=dma((2, NH, K)),
        tpf_r=dma((2, NH, K)),
        rsa_s=dma((2, NH)),
        rsa_r=dma((2, NH)),
        rsb_s=dma((2, NH, K)),
        rsb_r=dma((2, NH, K)),
        gr_s=dma((nst, 6)),
        gr_r=dma((nst, 6)),
        credit=pltpu.SemaphoreType.REGULAR((nst, 3)),
        home_s=dma((6, tz)),
        home_r=dma((6, max(TPN, C))),
        sig_s=dma((L, NH)),
        sig_r=dma((TPN,)),
        sm1_s=dma((TPN,)),
        sm1_rs=dma((TPN,)),
        sm2_s=dma((NU,)),
        sm2_rs=dma((NU,)),
        out_l=dma((L,)),
        smo_l=dma((1,)),
    )
    slots = 2 if nst == 2 else 1
    for m, block in mat_block.items():
        scratch["w%d" % m] = vm((LD if m in DECODER_MATS else L,) + two[m] + block, bf16)
        scratch["g%d" % m] = vm((slots,) + two[m] + block, bf16)
        scratch["st%d" % m] = vm((2 ** (len(two[m]) - nst),) + block, bf16)
        for j in range(1, nst + 1):
            scratch["r%d_%d" % (m, j)] = vm(two[m][j:] + block, bf16)
    in_names = ["src", "x2", "cot", "auxi", "dirwi", "normsi", "aq", "ai", "af", "ac", "woi", "wcoi"]
    out_names = ["out", "sig", "hq", "hi", "hf", "hc", "hwo", "hwco", "smout"]
    scratch_names = list(scratch)

    def kernel(*refs):
        n = types.SimpleNamespace(**dict(zip(in_names + out_names + scratch_names, refs)))
        W = {m: getattr(n, "w%d" % m) for m in mat_block}
        A = {QKV: n.aq, FIN: n.ai, FOUT: n.af, CQKV: n.ac}
        H = {QKV: n.hq, FIN: n.hi, FOUT: n.hf, CQKV: n.hc, OUT: n.hwo, COUT: n.hwco}
        G = {m: getattr(n, "g%d" % m) for m in mat_block}
        ST = {m: getattr(n, "st%d" % m) for m in mat_block}
        RB = {m: [None] + [getattr(n, "r%d_%d" % (m, j)) for j in range(1, nst + 1)] for m in mat_block}
        s, d = lax.axis_index("section"), lax.axis_index("dp")
        core, x = rm(s, 2), dv(s, 2)
        bit = [rm(dv(d, 1 << b), 2) for b in range(NB)]
        zl = bit[PAIR_BIT] if tz == 2 else 0
        k = zl * (NS // 2) + x
        r = core * K + k
        low = 1 << PAIR_BIT
        g = dv(d, 2 * low) * low + rm(d, low) if tz == 2 else d

        def place(rank, group):
            c2, k2 = dv(rank, K), rm(rank, K)
            x2, z2 = rm(k2, NS // 2), dv(k2, NS // 2)
            d2 = dv(group, low) * 2 * low + z2 * low + rm(group, low) if tz == 2 else group
            return (x2 * 2 + c2, d2)

        def with_bit(b, value):
            return d + (value - bit[b]) * (1 << b)

        def remote(src, dst, send, recv, device):
            return pltpu.make_async_remote_copy(
                src_ref=src, dst_ref=dst, send_sem=send, recv_sem=recv, device_id=device, device_id_type=MESH
            )

        def local(src, dst, sem):
            return pltpu.make_async_copy(src, dst, sem)

        def wait(ref, sem):
            pltpu.make_async_copy(ref, ref, sem).wait()

        sibling = place((1 - core) * K + k, g)

        barrier = pltpu.get_barrier_semaphore()
        total = NS * ND
        me = s * ND + d

        @pl.loop(1, total)
        def _(j):
            other = rm(me + j, total)
            pl.semaphore_signal(barrier, inc=1, device_id=(dv(other, ND), rm(other, ND)), device_id_type=MESH)

        pl.semaphore_wait(barrier, total - 1)

        own = pl.ds(mul(r, RR), RR)
        for j in range(1, NS):
            to = rm(s + j, NS)
            remote(n.normsi, n.norms.at[s], n.norm_s.at[j], n.norm_r.at[j], (to, d)).start()
        local(n.normsi, n.norms.at[s], n.norm_s.at[0]).start()
        other_rank = core * K + (1 - zl) * (NS // 2) + x
        other_rows = pl.ds(mul(other_rank, RR), RR)
        pair_dev = (s, with_bit(PAIR_BIT, 1 - zl)) if tz == 2 else None
        firsts = [
            (n.src, n.xbuf.at[0, zl], n.src, n.xbuf.at[0, zl]),
            (n.x2, n.xbuf.at[half + 1, zl], n.x2, n.xbuf.at[half + 1, zl]),
            (n.auxi, n.aux.at[zl], n.auxi, n.aux.at[zl]),
            (n.dirwi, n.dirw.at[zl], n.dirwi, n.dirw.at[zl]),
            (n.cot.at[own], n.cotb.at[zl], n.cot.at[other_rows], n.cotb.at[zl]),
        ]

        def first_start(i):
            a, b, c, e = firsts[i]
            local(a, b, n.init_l.at[i]).start()
            if tz == 2:
                remote(c, e, n.init_s.at[i], n.init_r.at[i], pair_dev).start()

        def first_wait(i):
            a, b, c, e = firsts[i]
            wait(b, n.init_l.at[i])
            if tz == 2:
                wait(e, n.init_s.at[i])
                wait(e, n.init_r.at[i])

        first_start(2)
        first_start(0)

        def wreg(m, l, fixed):
            idx = tuple(fixed.get(b, slice(None)) for b in mat_bits[m])
            return W[m].at[(l - half if m in DECODER_MATS else l,) + idx]

        mine = {b: bit[b] for b in range(NB)}

        def a2a_start(m):
            dst = wreg(m, s, mine)
            local(A[m].at[r], dst, n.a2a_r.at[m, s, zl]).start()
            for j in range(1, TPN):
                to = rm(r + j, TPN)
                remote(A[m].at[to], dst, n.a2a_s.at[m, j], n.a2a_r.at[m, s, zl], place(to, g)).start()

        def group_bits(m, group):
            count = len(mat_bits[m])
            return tuple(rm(dv(group, 1 << (count - 1 - i)), 2) for i in range(count))

        def out_pieces(m):
            rank = dv(d, q)
            for c in range(C):
                group = rm(d, q) * C + c
                yield c, pl.ds(c * cw, cw), group, rank, (rank == r) & (group == g)

        def out_start(m, src):
            for c, span, group, rank, here in out_pieces(m):
                dst = W[m].at[(s - half if m in DECODER_MATS else s,) + group_bits(m, group)]

                @pl.when(here)
                def _():
                    local(src.at[:, span], dst, n.a2a_r.at[m, s, 0]).start()

                @pl.when(jnp.logical_not(here))
                def _():
                    remote(src.at[:, span], dst, n.wo_s.at[m - OUT, c], n.a2a_r.at[m, s, 0], place(rank, group)).start()

        def kind_layer(t):
            td = jnp.maximum(t - 2 * half, 0)
            is_enc = t < 2 * half
            tt = jnp.maximum(t, 0)
            kind = jnp.where(is_enc, 2 * rm(tt, 2), rm(td, 3))
            layer = jnp.where(is_enc, dv(tt, 2), half + dv(td, 3))
            return kind, layer

        def groups(t, fn, after_kind=None):
            valid = (t >= 0) & (t < T)
            kind, layer = kind_layer(t)
            for kd, mats in KIND_MATS.items():

                @pl.when(valid & (kind == kd))
                def _():
                    fn(kd, mats, layer)

        def ag_region(j, m, l, flip):
            fixed = {b: bit[b] for b in p.steps[j:]}
            if flip:
                fixed[p.steps[j]] = 1 - bit[p.steps[j]]
            return wreg(m, l, fixed)

        def ag_start(j, m, l):
            reg = ag_region(j, m, l, False)
            to = (s, with_bit(p.steps[j], 1 - bit[p.steps[j]]))
            remote(reg, reg, n.ag_s.at[j, m, l], n.ag_r.at[j, m, l], to).start()

        def ag_wait(j, m, l):
            if j == 0 and m in (OUT, COUT):
                wait(wreg(m, l, mine), n.a2a_r.at[m, l, 0])
            elif j == 0:
                for z in range(tz):
                    fixed = dict(mine)
                    if tz == 2:
                        fixed[PAIR_BIT] = z
                    wait(wreg(m, l, fixed), n.a2a_r.at[m, l, z])
            else:
                wait(ag_region(j - 1, m, l, True), n.ag_r.at[j - 1, m, l])

        ahead = AHEAD if nst == 2 else tuple(range(nst + 1, 0, -1))

        def feed(t):
            def fn0(kd, mats, l):
                @pl.when(l == s)
                def _():
                    for m in mats:
                        if m == OUT:
                            out_start(OUT, n.woi)
                        elif m == COUT:
                            out_start(COUT, n.wcoi)
                        else:
                            a2a_start(m)

            groups(t + ahead[0], fn0)
            for j in range(1, nst + 1):

                def fn(kd, mats, l, j=j):
                    for m in mats:
                        ag_wait(j - 1, m, l)
                    for m in mats:
                        ag_start(j - 1, m, l)

                groups(t + ahead[j], fn)

        def ready(t):
            def last(kd, mats, l):
                for m in mats:
                    ag_wait(nst, m, l)

            groups(t, last)

        @pl.loop(0, ahead[0])
        def _(i):
            feed(i - ahead[0])

        first_start(1)
        first_start(4)
        first_start(3)

        def tp_start(buf, h, st=0):
            mine_rows = buf.at[own]
            for j in range(1, K):
                k2 = rm(k + j, K)
                remote(mine_rows, mine_rows, n.tpa_s.at[st, h, j], n.tpa_r.at[st, h, j], place(core * K + k2, g)).start()
            remote(mine_rows, mine_rows, n.tpa_s.at[st, h, 0], n.tpa_r.at[st, h, 0], sibling).start()

        def tp_finish(buf, h, st=0):
            def rows(c2, k2):
                return buf.at[pl.ds(mul(c2 * K + k2, RR), RR)]

            for j in range(1, K):
                k2 = rm(k - j + K, K)
                ref = rows(core, k2)
                wait(ref, n.tpa_r.at[st, h, j])
                remote(ref, ref, n.tpf_s.at[st, h, j], n.tpf_r.at[st, h, j], sibling).start()
            wait(rows(1 - core, k), n.tpa_r.at[st, h, 0])
            for j in range(1, K):
                wait(rows(1 - core, rm(k - j + K, K)), n.tpf_r.at[st, h, j])
            for j in range(K):
                wait(rows(core, k), n.tpa_s.at[st, h, j])
            for j in range(1, K):
                wait(rows(core, rm(k - j + K, K)), n.tpf_s.at[st, h, j])

        def rs_start(st, h, partial):
            n.rsas[st, h] = partial(mul(1 - core, HB)).astype(bf16)
            copy = remote(n.rsas.at[st, h], n.rsar.at[st, h], n.rsa_s.at[st, h], n.rsa_r.at[st, h], sibling)
            copy.start()
            n.rsp[h] = partial(mul(core, HB))
            wait(n.rsar.at[st, h], n.rsa_r.at[st, h])
            for j in range(1, K):
                k2 = rm(k + j, K)
                rows = pl.ds(mul(k2, RR), RR)
                n.rsbs[st, h, j] = (n.rsp[h, rows] + n.rsar[st, h, rows].astype(f32)).astype(bf16)
                remote(
                    n.rsbs.at[st, h, j],
                    n.rsbr.at[st, h, j],
                    n.rsb_s.at[st, h, j],
                    n.rsb_r.at[st, h, j],
                    place(core * K + k2, g),
                ).start()
            rows = pl.ds(mul(k, RR), RR)
            n.rsp[h, rows] = n.rsp[h, rows] + n.rsar[st, h, rows].astype(f32)
            wait(n.rsas.at[st, h], n.rsa_s.at[st, h])

        def rs_finish(st, h):
            acc = n.rsp[h, pl.ds(mul(k, RR), RR)]
            for j in range(1, K):
                wait(n.rsbr.at[st, h, j], n.rsb_r.at[st, h, j])
                acc = acc + n.rsbr[st, h, j].astype(f32)
            for j in range(1, K):
                wait(n.rsbs.at[st, h, j], n.rsb_s.at[st, h, j])
            return acc

        def halves(fn):
            if NH == 1:
                fn(0)
            else:
                pl.loop(0, NH)(fn)

        def weight(m, l, lo=0, hi=None):
            hi = mat_block[m][1] if hi is None else hi
            at = (l - half if m in DECODER_MATS else l,) + (slice(None),) * (NB + 1) + (slice(lo, hi),)
            return W[m][at].reshape((-1, hi - lo))

        def out_weight(m, l, c):
            parts = [W[m][(l - half if m in DECODER_MATS else l,) + group_bits(m, a * C + c)] for a in range(q)]
            return parts[0] if q == 1 else jnp.concatenate(parts, axis=0)

        def out_product(rows, m, l):
            return jnp.concatenate([dot(rows, out_weight(m, l, c), NN) for c in range(C)], axis=1)

        def out_product_back(grad, m, l):
            acc = None
            for c in range(C):
                term = dot(grad[:, c * cw : (c + 1) * cw], out_weight(m, l, c), NT)
                acc = term if acc is None else acc + term
            return acc

        def norm_row(l, row):
            return n.norms[l][row : row + 1, :]

        def ln_forward(t, h, value, gain, bias):
            centre = value - jnp.mean(value, axis=-1, keepdims=True)
            scale = lax.rsqrt(jnp.mean(centre * centre, axis=-1, keepdims=True) + EPSILON)
            z = centre * scale
            n.zs[t, h] = z.astype(bf16)
            n.rstd[t, h] = jnp.broadcast_to(scale, (RR, 128))
            return z * gain + bias

        def ln_backward(t, h, grad, l, gain_row, bias_row):
            z = n.zs[t, h].astype(f32)
            scale = n.rstd[t, h][:, :1]
            n.small[l, gain_row : gain_row + 1, :] += jnp.sum(grad * z, axis=0, keepdims=True)
            n.small[l, bias_row : bias_row + 1, :] += jnp.sum(grad, axis=0, keepdims=True)
            gz = grad * norm_row(l, gain_row)
            return scale * (
                gz - jnp.mean(gz, axis=-1, keepdims=True) - z * jnp.mean(gz * z, axis=-1, keepdims=True)
            )

        head_width = D // HEADS
        score_scale = 1.0 / math.sqrt(head_width)

        def allowed_of(h, causal):
            rows = lax.broadcasted_iota(jnp.int32, (R, R), 0)
            cols = lax.broadcasted_iota(jnp.int32, (R, R), 1)
            ok = (dv_vec(rows) == dv_vec(cols)) & (n.aux[h][1:2] > 0.5 if causal else n.aux[h][0:1] > 0.5)
            return ok & (cols <= rows) if causal else ok

        def dv_vec(v):
            return lax.div(v, jnp.full_like(v, p.seq))

        def head_lanes(head):
            lane = lax.broadcasted_iota(jnp.int32, (1, CW), 1)
            return (lane >= head * head_width) & (lane < (head + 1) * head_width)

        def only(value, head):
            return jnp.where(head_lanes(head), value, jnp.zeros_like(value))

        def probabilities(qs, ks, allowed, head):
            scores = dot(only(qs, head), ks, NT) * score_scale
            scores = jnp.where(allowed, scores, MASKED)
            e = jnp.exp(scores - jnp.max(scores, axis=-1, keepdims=True))
            return e / jnp.sum(e, axis=-1, keepdims=True)

        def attend(qs, ks, vs, allowed):
            out = jnp.zeros((R, CW), f32)
            for head in range(p.HPR):
                probs = probabilities(qs, ks, allowed, head)
                out = out + only(dot(probs.astype(bf16), vs, NN), head)
            return out.astype(bf16)

        def attend_back(qs, ks, vs, allowed, grad):
            gq = gk = gv = jnp.zeros((R, CW), f32)
            for head in range(p.HPR):
                probs = probabilities(qs, ks, allowed, head)
                gp = dot(only(grad, head), vs, NT)
                gs = (probs * (gp - jnp.sum(gp * probs, axis=-1, keepdims=True))).astype(bf16)
                gv = gv + only(dot(probs.astype(bf16), grad, TN), head)
                gq = gq + only(dot(gs, ks, NN), head)
                gk = gk + only(dot(gs, qs, TN), head)
            return (gq * score_scale).astype(bf16), (gk * score_scale).astype(bf16), gv.astype(bf16)

        def split3(value):
            return value[:, :CW], value[:, CW : 2 * CW], value[:, 2 * CW :]

        c0, c1 = math.sqrt(2.0 / math.pi), 0.044715

        def gelu(v):
            return 0.5 * v * (1.0 + jnp.tanh(c0 * (v + c1 * (v * v * v))))

        def gelu_slope(v):
            th = jnp.tanh(c0 * (v + c1 * (v * v * v)))
            return 0.5 * (1.0 + th) + 0.5 * v * (1.0 - th * th) * (c0 * (1.0 + 3.0 * c1 * v * v))

        def self_forward(l, t, xi, causal, alpha, into):
            feed(t)
            ready(t)

            def first(h):
                n.qkv[l, h] = dot(n.xbuf[xi, h], weight(QKV, l), NN).astype(bf16)
                qs, ks, vs = split3(n.qkv[l, h])
                n.osv[l, h] = attend(qs, ks, vs, allowed_of(h, causal))
                rs_start(0, h, lambda row: out_product(n.osv[l, h, pl.ds(row, HB)], OUT, l))

            def second(h):
                value = alpha * n.xbuf[xi, h, own].astype(f32) + rs_finish(0, h)
                hidden = ln_forward(t, h, value, norm_row(l, 0), norm_row(l, 2))
                n.res[h] = hidden
                into[h, own] = hidden.astype(bf16)
                tp_start(into.at[h], h)

            halves(first)
            halves(second)

        def cross_forward(l, t):
            feed(t)
            ready(t)
            ld = l - half

            def first(h):
                n.cqkv[ld, h, :, CW:] = dot(n.xbuf[half, h], weight(CQKV, l, CW), NN).astype(bf16)
                tp_finish(n.h1b.at[ld, h], h)
                n.cqkv[ld, h, :, :CW] = dot(n.h1b[ld, h], weight(CQKV, l, 0, CW), NN).astype(bf16)
                qs, ks, vs = split3(n.cqkv[ld, h])
                n.cosv[ld, h] = attend(qs, ks, vs, allowed_of(h, False))
                rs_start(0, h, lambda row: out_product(n.cosv[ld, h, pl.ds(row, HB)], COUT, l))

            def second(h):
                value = DECODER_ALPHA * n.res[h] + rs_finish(0, h)
                hidden = ln_forward(t, h, value, norm_row(l, 4), norm_row(l, 5))
                n.res[h] = hidden
                n.hb[l, h, own] = hidden.astype(bf16)
                tp_start(n.hb.at[l, h], h)

            halves(first)
            halves(second)

        def ffn_forward(l, t, xo, alpha):
            feed(t)
            ready(t)

            def first(h):
                tp_finish(n.hb.at[l, h], h)
                before = dot(n.hb[l, h], weight(FIN, l), NN)
                n.pre[l, h] = before.astype(bf16)
                n.act[...] = gelu(before).astype(bf16)
                rs_start(0, h, lambda row: dot(n.act[pl.ds(row, HB)], weight(FOUT, l), NN))

            def second(h):
                value = alpha * n.res[h] + rs_finish(0, h)
                result = ln_forward(t, h, value, norm_row(l, 1), norm_row(l, 3))
                n.xbuf[xo, h, own] = result.astype(bf16)
                tp_start(n.xbuf.at[xo, h], h, 1)

            def third(h):
                tp_finish(n.xbuf.at[xo, h], h, 1)

            halves(first)
            halves(second)
            halves(third)

            @pl.when(s == l)
            def _():
                local(n.xbuf.at[xo, zl], n.out, n.out_l.at[0]).start()

        for i in (2, 0):
            first_wait(i)
        for j in range(1, NS):
            wait(n.norms.at[rm(s - j + NS, NS)], n.norm_r.at[j])
        wait(n.norms.at[s], n.norm_s.at[0])
        n.small[...] = jnp.zeros_like(n.small)
        n.gmem[...] = jnp.zeros_like(n.gmem)

        @pl.loop(0, half)
        def _(l):
            self_forward(l, 2 * l, l, False, ENCODER_ALPHA, n.hb.at[l])
            ffn_forward(l, 2 * l + 1, l + 1, ENCODER_ALPHA)

        for i in (1, 3, 4):
            first_wait(i)

        @pl.loop(half, L)
        def _(l):
            t = 2 * half + 3 * (l - half)
            self_forward(l, t, l + 1, True, DECODER_ALPHA, n.h1b.at[l - half])
            cross_forward(l, t + 1)
            ffn_forward(l, t + 2, l + 2, DECODER_ALPHA)

        def gbuf(m, l):
            return G[m].at[rm(l, slots)]

        def gregion(m, l, fixed):
            return gbuf(m, l).at[tuple(fixed.get(b, slice(None)) for b in mat_bits[m])]

        def partner(j):
            b = back_steps[j - 1]
            return (s, with_bit(b, 1 - bit[b]))

        def gr_start(j, kd, mats, l):
            @pl.when(l != L - 1)
            def _():
                pl.semaphore_wait(n.credit.at[j - 1, kd], 1)

            for m in mats:
                fixed = {b: bit[b] for b in back_steps[: j - 1]}
                fixed[back_steps[j - 1]] = 1 - bit[back_steps[j - 1]]
                remote(
                    gregion(m, l, fixed), RB[m][j], n.gr_s.at[j - 1, m], n.gr_r.at[j - 1, m], partner(j)
                ).start()

        def blocks_of(count):
            return [
                tuple((i >> b) & 1 for b in reversed(range(count))) for i in range(1 << count)
            ]

        def gr_finish(j, kd, mats, l):
            for m in mats:
                wait(RB[m][j], n.gr_r.at[j - 1, m])
                mine_part = gregion(m, l, {b: bit[b] for b in back_steps[:j]})
                for idx in blocks_of(len(mat_bits[m]) - j):
                    value = mine_part[idx].astype(f32) + RB[m][j][idx].astype(f32)
                    if j == nst:
                        ST[m][idx if idx else 0] = value.astype(bf16)
                    else:
                        mine_part[idx] = value.astype(bf16)
                wait(RB[m][j], n.gr_s.at[j - 1, m])

            @pl.when(l != (half if kd == CROSS else 0))
            def _():
                pl.semaphore_signal(n.credit.at[j - 1, kd], inc=1, device_id=partner(j), device_id_type=MESH)

        def home(m, l, z, act):
            src = ST[m].at[z]
            if m in (OUT, COUT):
                piece = rm(g, C)
                to = (l, r * q + dv(g, C))
                here = (l == s) & (to[1] == d)
                dst, slot = H[m].at[:, pl.ds(mul(piece, cw), cw)], piece
            else:
                to = (l, with_bit(PAIR_BIT, z) if tz == 2 else d)
                here = (l == s) & (zl == z) if tz == 2 else l == s
                dst, slot = H[m].at[r], r

            if act == "wait":
                wait(src, n.home_s.at[m, z])
                return

            @pl.when(here)
            def _():
                local(src, dst, n.home_s.at[m, z]).start()

            @pl.when(jnp.logical_not(here))
            def _():
                remote(src, dst, n.home_s.at[m, z], n.home_r.at[m, slot], to).start()

        behind = BEHIND if nst == 2 else tuple(range(1, nst + 1))

        def process(u):
            def old(kd, mats, l):
                for m in mats:
                    for z in range(ST[m].shape[0]):
                        home(m, l, z, "wait")

            groups(T - 1 - (u - behind[nst - 1] - 1), old)
            for j in range(nst, 0, -1):

                def fn(kd, mats, l, j=j):
                    gr_finish(j, kd, mats, l)
                    if j < nst:
                        gr_start(j + 1, kd, mats, l)
                    else:
                        for m in mats:
                            for z in range(ST[m].shape[0]):
                                home(m, l, z, "start")

                groups(T - 1 - (u - behind[j - 1]), fn)

        def weight_grad(m, l, lefts, rights):
            rows, cols = mat_block[m]
            count = max(1, 128 // rows)
            tile = rows * count

            @pl.loop(0, ND // count)
            def _(i):
                span = pl.ds(mul(i, tile), tile)
                parts = []
                for left, right in zip(lefts, rights):
                    acc = None
                    for h in range(NH):
                        term = dot(left[h][:, span], right[h][...], TN)
                        acc = term if acc is None else acc + term
                    parts.append(acc)
                value = parts[0] if len(parts) == 1 else jnp.concatenate(parts, axis=1)
                value = value.astype(bf16)
                for e in range(count):
                    at = i * count + e
                    idx = tuple(rm(dv(at, 1 << b), 2) for b in reversed(range(NB)))
                    gbuf(m, l)[idx] = value[e * rows : (e + 1) * rows]

        def out_grad(m, l, left, right):
            for c in range(C):
                acc = None
                for h in range(NH):
                    term = dot(left[h][...], right[h][:, c * cw : (c + 1) * cw], TN)
                    acc = term if acc is None else acc + term
                acc = acc.astype(bf16)
                for a in range(q):
                    gbuf(m, l)[group_bits(m, a * C + c)] = acc[a * p.rb : (a + 1) * p.rb]

        def each(ref):
            return [ref.at[h] for h in range(NH)]

        def branch_grad(t, l, u, gain_row, bias_row):
            gag = n.gag.at[rm(u, 2)]

            def fn(h):
                grad = ln_backward(t, h, n.gy[h], l, gain_row, bias_row)
                n.res[h] = grad
                gag[h, own] = grad.astype(bf16)
                tp_start(gag.at[h], h)

            halves(fn)
            return gag

        def ffn_backward(l, t, u, alpha):
            gag = branch_grad(t, l, u, 1, 3)

            def first(h):
                tp_finish(gag.at[h], h)
                before = n.pre[l, h].astype(f32)
                gact = dot(gag[h], weight(FOUT, l), NT)
                n.gpre[h] = (gact * gelu_slope(before)).astype(bf16)
                rs_start(0, h, lambda row: dot(n.gpre[h, pl.ds(row, HB)], weight(FIN, l), NT))
                n.actb[h] = gelu(before).astype(bf16)

            halves(first)
            process(u)
            weight_grad(FOUT, l, [each(n.actb)], [each(gag)])
            weight_grad(FIN, l, [each(n.hb.at[l])], [each(n.gpre)])
            gr_start(1, FFN, KIND_MATS[FFN], l)

            def second(h):
                n.gy[h] = alpha * n.res[h] + rs_finish(0, h)

            halves(second)

        def cross_backward(l, t, u):
            gag = branch_grad(t, l, u, 4, 5)
            ld = l - half

            def first(h):
                tp_finish(gag.at[h], h)
                grad = out_product_back(gag.at[h], COUT, l).astype(bf16)
                qs, ks, vs = split3(n.cqkv[ld, h])
                gq, gk, gv = attend_back(qs, ks, vs, allowed_of(h, False), grad)
                n.gqkv[h, :, :CW] = gq
                n.gqkv[h, :, CW : 2 * CW] = gk
                n.gqkv[h, :, 2 * CW :] = gv
                rs_start(
                    0, h, lambda row: dot(n.gqkv[h, pl.ds(row, HB), :CW], weight(CQKV, l, 0, CW), NT)
                )
                n.gmem[h] += dot(n.gqkv[h, :, CW:], weight(CQKV, l, CW), NT)

            halves(first)
            process(u)
            out_grad(COUT, l, each(n.cosv.at[ld]), each(gag))
            weight_grad(
                CQKV,
                l,
                [each(n.h1b.at[ld]), each(n.xbuf.at[half])],
                [
                    [n.gqkv.at[h, :, pl.ds(0, CW)] for h in range(NH)],
                    [n.gqkv.at[h, :, pl.ds(CW, 2 * CW)] for h in range(NH)],
                ],
            )
            gr_start(1, CROSS, KIND_MATS[CROSS], l)

            def second(h):
                n.gy[h] = DECODER_ALPHA * n.res[h] + rs_finish(0, h)

            halves(second)

        def sig_copy(l, h, act):
            here = (l == s) & (h == zl)
            src = n.gxo.at[l, h]

            @pl.when(here)
            def _():
                if act == "start":
                    local(src, n.sig.at[own], n.sig_r.at[r]).start()

            @pl.when(jnp.logical_not(here))
            def _():
                if act == "start":
                    to = (l, with_bit(PAIR_BIT, h) if tz == 2 else d)
                    remote(src, n.sig.at[own], n.sig_s.at[l, h], n.sig_r.at[r], to).start()
                else:
                    wait(src, n.sig_s.at[l, h])

        def self_backward(l, t, u, xi, causal, alpha):
            gag = branch_grad(t, l, u, 0, 2)

            def first(h):
                tp_finish(gag.at[h], h)
                grad = out_product_back(gag.at[h], OUT, l).astype(bf16)
                qs, ks, vs = split3(n.qkv[l, h])
                gq, gk, gv = attend_back(qs, ks, vs, allowed_of(h, causal), grad)
                n.gqkv[h, :, :CW] = gq
                n.gqkv[h, :, CW : 2 * CW] = gk
                n.gqkv[h, :, 2 * CW :] = gv
                rs_start(0, h, lambda row: dot(n.gqkv[h, pl.ds(row, HB)], weight(QKV, l), NT))

            halves(first)
            process(u)
            out_grad(OUT, l, each(n.osv.at[l]), each(gag))
            weight_grad(QKV, l, [each(n.xbuf.at[xi])], [each(n.gqkv)])
            gr_start(1, ATTN, KIND_MATS[ATTN], l)

            def second(h):
                grad = (alpha * n.res[h] + rs_finish(0, h)).astype(bf16)
                n.gxo[l, h] = grad
                n.gy[h] = grad.astype(f32)
                sig_copy(l, h, "start")

            halves(second)

        def seed(h):
            n.gy[h] = n.cotb[h].astype(f32)

        halves(seed)

        @pl.loop(0, LD)
        def _(i):
            l = L - 1 - i
            t = 2 * half + 3 * (l - half)
            ffn_backward(l, t + 2, 3 * i, DECODER_ALPHA)
            cross_backward(l, t + 1, 3 * i + 1)
            self_backward(l, t, 3 * i + 2, l + 1, True, DECODER_ALPHA)

        def directions(h):
            column = n.dirw[h, dv(r * RR, p.seq)][:, :1]
            rows = column * jnp.sum(n.gy[h], axis=0, keepdims=True)
            for sec in range(NS):
                lo = sec * p.dir_rows
                n.small[sec, 8 : 8 + p.dir_rows, :] += rows[lo : lo + p.dir_rows]

        halves(directions)

        def memory_first(h):
            rs_start(1, h, lambda row: n.gmem[h, pl.ds(row, HB)])

        def memory_second(h):
            n.gy[h] = rs_finish(1, h).astype(bf16).astype(f32)

        halves(memory_first)
        halves(memory_second)

        @pl.loop(0, half)
        def _(i):
            l = half - 1 - i
            u = 3 * LD + 2 * i
            ffn_backward(l, 2 * l + 1, u, ENCODER_ALPHA)
            self_backward(l, 2 * l, u + 1, l, False, ENCODER_ALPHA)

        for rank in range(TPN):
            for g2 in range(NU):
                sec, d2 = place(rank, g2)
                lo = d2 * p.cols
                tile, lane = divmod(g2 * p.cols, 128)
                n.sm1[rank, tile, :, lane : lane + p.cols] = n.small[sec, :, lo : lo + p.cols]
        for j in range(1, TPN):
            to = rm(r + j, TPN)
            remote(n.sm1.at[to], n.sm1r.at[j], n.sm1_s.at[j], n.sm1_rs.at[j], place(to, g)).start()

        @pl.loop(0, behind[nst - 1] + 1)
        def _(i):
            process(T + i)

        total_small = n.sm1[r]
        for j in range(1, TPN):
            wait(n.sm1r.at[j], n.sm1_rs.at[j])
            total_small = total_small + n.sm1r[j]
        for g2 in range(NU):
            tile, lane = divmod(g2 * p.cols, 128)
            n.sm2[g2, :, : p.cols] = total_small[tile, :, lane : lane + p.cols]
        for j in range(1, NU):
            to = rm(g + j, NU)
            remote(n.sm2.at[to], n.sm2r.at[j], n.sm2_s.at[j], n.sm2_rs.at[j], place(r, to)).start()
        mine_small = n.sm2[g]
        for j in range(1, NU):
            wait(n.sm2r.at[j], n.sm2_rs.at[j])
            mine_small = mine_small + n.sm2r[j]
        n.smo[...] = mine_small
        local(n.smo, n.smout, n.smo_l.at[0]).start()
        wait(n.smo, n.smo_l.at[0])

        def home_wait(m):
            for j in range(1, TPN):
                rank = rm(r + j, TPN)
                wait(H[m].at[rank], n.home_r.at[m, rank])

        def home_wait_out(m):
            for c, span, group, rank, here in out_pieces(m):

                @pl.when(jnp.logical_not(here))
                def _():
                    wait(H[m].at[:, span], n.home_r.at[m, c])

        for m in (QKV, FIN, FOUT):
            home_wait(m)
        home_wait_out(OUT)

        @pl.when(s >= half)
        def _():
            home_wait(CQKV)
            home_wait_out(COUT)

        for rank in range(TPN):
            wait(n.sig.at[pl.ds(rank * RR, RR)], n.sig_r.at[rank])
        wait(n.out, n.out_l.at[0])
        for l in range(L):
            for h in range(NH):
                sig_copy(l, h, "wait")
        for j in range(1, TPN):
            wait(n.sm1.at[0], n.sm1_s.at[j])
        for j in range(1, NU):
            wait(n.sm2.at[0], n.sm2_s.at[j])
        for j in range(1, NS):
            wait(n.norms.at[0], n.norm_s.at[j])
        for j in range(1, TPN):
            for m in (QKV, FIN, FOUT):
                wait(A[m].at[0], n.a2a_s.at[m, j])

        @pl.when(s >= half)
        def _():
            for j in range(1, TPN):
                wait(A[CQKV].at[0], n.a2a_s.at[CQKV, j])

        for m in (OUT, COUT):
            for c, span, group, rank, here in out_pieces(m):
                sends = jnp.logical_not(here) if m == OUT else jnp.logical_not(here) & (s >= half)

                @pl.when(sends)
                def _():
                    wait(n.woi.at[:, span], n.wo_s.at[m - OUT, c])

        @pl.loop(0, L)
        def _(l):
            for j in range(nst):
                for m in mat_block:
                    if m not in DECODER_MATS:
                        wait(ag_region(j, m, l, False), n.ag_s.at[j, m, l])

                @pl.when(l >= half)
                def _():
                    for m in DECODER_MATS:
                        wait(ag_region(j, m, l, False), n.ag_s.at[j, m, l])

    def sd(*shape, dtype=bf16):
        return jax.ShapeDtypeStruct(shape, dtype)

    def blocks(m, lead):
        return sd(lead, *mat_block[m])

    outs = [
        sd(R, D),
        sd(R, D),
        blocks(QKV, TPN),
        blocks(FIN, TPN),
        blocks(FOUT, TPN),
        blocks(CQKV, TPN),
        sd(p.rb, D),
        sd(p.rb, D),
        sd(16, 128, dtype=f32),
    ]
    anywhere = pl.BlockSpec(memory_space=pl.ANY)
    return pl.pallas_call(
        kernel,
        out_shape=outs,
        in_specs=[anywhere] * len(in_names),
        out_specs=[anywhere] * len(out_names),
        scratch_shapes=list(scratch.values()),
        compiler_params=pltpu.CompilerParams(
            collective_id=0, has_side_effects=True, vmem_limit_bytes=64 * 1024 * 1024 - 64 * 1024
        ),
    )


def solution(mesh):
    def body(
        source,
        target,
        directions,
        source_lengths,
        target_lengths,
        attn_in,
        attn_out,
        ffn_in,
        ffn_out,
        cross_weight,
        norm_gain,
        norm_bias,
        cross_norm,
        dir_table,
        cotangent,
    ):
        pairs, seq, width = source.shape
        p = make_plan(
            mesh.shape["section"], mesh.shape["dp"], pairs, seq, width, ffn_in.shape[2], dir_table.shape[0]
        )
        section = lax.axis_index("section")
        routing = (directions[:, None] == jnp.arange(p.NDIR)[None, :]).astype(f32)
        rows = jnp.dot(routing, dir_table, precision=lax.Precision.HIGHEST)
        x2 = (target.astype(f32) + rows[:, None, :]).astype(bf16).reshape(p.R, width)
        positions = jnp.arange(seq)
        valid = [(positions[None, :] < lens[:, None]).astype(f32).reshape(1, p.R) for lens in (source_lengths, target_lengths)]
        aux = jnp.concatenate(valid + [jnp.zeros((6, p.R), f32)], axis=0)
        dirw = jnp.broadcast_to(routing[:, :, None], (pairs, p.NDIR, 128))
        norms = jnp.concatenate(
            (norm_gain[0], norm_bias[0], cross_norm[0], jnp.zeros((2, width), bf16)), axis=0
        ).astype(f32)
        aq = attn_in[0].reshape(p.rb, 3, p.TPN, p.CW).transpose(2, 0, 1, 3).reshape(p.TPN, p.rb, 3 * p.CW)
        cross = cross_weight[0][:, : 3 * width]
        ac = cross.reshape(p.rb, 3, p.TPN, p.CW).transpose(2, 0, 1, 3).reshape(p.TPN, p.rb, 3 * p.CW)
        ai = ffn_in[0].reshape(p.rb, p.ND, p.TPN, p.fb).transpose(2, 0, 1, 3).reshape(p.TPN, p.rb, p.FB)
        af = ffn_out[0].reshape(p.TPN, p.fb, width)
        out, sig, hq, hi, hf, hc, hwo, hwco, small = build(p)(
            source.reshape(p.R, width),
            x2,
            cotangent.reshape(p.R, width),
            aux,
            dirw,
            norms,
            aq,
            ai,
            af,
            ac,
            attn_out[0],
            cross_weight[0][:, 3 * width :],
        )
        decoder = section >= p.half

        def heads_back(value):
            value = value.reshape(p.TPN, p.rb, 3, p.CW).transpose(1, 2, 0, 3)
            return value.reshape(1, p.rb, 3 * width).astype(f32)

        g_in = hi.reshape(p.TPN, p.rb, p.ND, p.fb).transpose(1, 2, 0, 3).reshape(1, p.rb, p.FF).astype(f32)
        g_out = hf.reshape(1, p.TPN * p.fb, width).astype(f32)
        g_wo = hwo.astype(f32)[None]
        g_cross = jnp.concatenate((heads_back(hc), hwco.astype(f32)[None]), axis=2)
        g_cross = jnp.where(decoder, g_cross, jnp.zeros_like(g_cross))
        small = small[:, : p.cols]
        return (
            out.reshape(1, pairs, seq, width),
            sig.reshape(1, pairs, seq, width),
            heads_back(hq),
            g_wo,
            g_in,
            g_out,
            g_cross,
            small[None, 0:2],
            small[None, 2:4],
            small[None, 4:6],
            small[8 : 8 + p.dir_rows],
        )

    sharded = P("section", "dp", None)
    return jax.shard_map(
        body,
        mesh=mesh,
        in_specs=(
            P("dp", None, None),
            P("dp", None, None),
            P("dp"),
            P("dp"),
            P("dp"),
            sharded,
            sharded,
            sharded,
            sharded,
            sharded,
            P("section", None, None),
            P("section", None, None),
            P("section", None, None),
            P(),
            P("dp", None, None),
        ),
        out_specs=(
            P("section", "dp", None, None),
            P("section", "dp", None, None),
            sharded,
            sharded,
            sharded,
            sharded,
            sharded,
            P("section", None, "dp"),
            P("section", None, "dp"),
            P("section", None, "dp"),
            P("section", "dp"),
        ),
        check_vma=False,
    )
```

```python
import math
import types

import jax
import jax.numpy as jnp
from jax import lax
from jax.experimental import pallas as pl
from jax.experimental.pallas import tpu as pltpu
from jax.sharding import PartitionSpec as P

HEADS = 16
GROUP = 8
AHEAD = (4, 3, 2)
BEHIND = (2, 3)
PAIR_BIT = 0
ENCODER_ALPHA = 3.42
DECODER_ALPHA = 4.16
MASKED = -1000000000.0
EPSILON = 1e-05
MESH = pl.DeviceIdType.MESH
f32, bf16 = jnp.float32, jnp.bfloat16
NN, NT, TN = (((1,), (0,)), ((), ())), (((1,), (1,)), ((), ())), (((0,), (0,)), ((), ()))
ATTN, CROSS, FFN = 0, 1, 2
QKV, FIN, FOUT, CQKV, OUT, COUT = range(6)
KIND_MATS = {ATTN: (QKV, OUT), CROSS: (CQKV, COUT), FFN: (FOUT, FIN)}
DECODER_MATS = (CQKV, COUT)


def dot(a, b, dims):
    return lax.dot_general(a, b, dims, preferred_element_type=f32)


def dv(a, b):
    return a // b if isinstance(a, int) else lax.div(a, jnp.int32(b))


def rm(a, b):
    return a % b if isinstance(a, int) else lax.rem(a, jnp.int32(b))


def mul(a, b):
    return pl.multiple_of(a * b, b)


def make_plan(sections, dp_count, pairs, seq, width, ff, directions):
    p = types.SimpleNamespace()
    p.NS, p.ND, p.L, p.half = sections, dp_count, sections, sections // 2
    p.pairs, p.seq, p.D, p.FF, p.R = pairs, seq, width, ff, pairs * seq
    p.tz = 2 if sections < GROUP and dp_count >= 4 else 1
    p.TPN = sections * p.tz
    p.K = p.TPN // 2
    p.RR = p.R // p.TPN
    p.CW = width // p.TPN
    p.HPR = HEADS // p.TPN
    p.FB = ff // p.TPN
    p.rb = width // dp_count
    p.fb = ff // dp_count // p.TPN
    p.q = dp_count // p.TPN
    p.NU = dp_count // p.tz
    p.C = p.NU // p.q
    p.cw = width // p.C
    p.NB = dp_count.bit_length() - 1
    if p.tz == 2:
        p.steps = [b for b in reversed(range(p.NB)) if b != PAIR_BIT]
    else:
        p.steps = list(range(p.NB))
    p.nst = len(p.steps)
    p.T = 2 * p.half + 3 * (p.L - p.half)
    p.NDIR = directions
    p.dir_rows = directions // sections
    p.cols = width // dp_count
    return p


def build(p):
    NS, ND, L, half, TPN, K, RR, R, D = p.NS, p.ND, p.L, p.half, p.TPN, p.K, p.RR, p.R, p.D
    CW, FB, NU, NB, nst, T, tz, q = p.CW, p.FB, p.NU, p.NB, p.nst, p.T, p.tz, p.q
    NH, LD = tz, p.L - p.half
    HB = K * RR
    C, cw = p.C, p.cw
    mat_block = {
        QKV: (p.rb, 3 * CW),
        FIN: (p.rb, FB),
        FOUT: (p.fb, D),
        CQKV: (p.rb, 3 * CW),
        OUT: (p.rb, cw),
        COUT: (p.rb, cw),
    }
    all_bits = list(reversed(range(NB)))
    mat_bits = {m: [b for b in all_bits if b in p.steps] if m in (OUT, COUT) else all_bits for m in mat_block}
    two = {m: (2,) * len(mat_bits[m]) for m in mat_block}
    back_steps = p.steps[::-1]

    vm, dma = pltpu.VMEM, pltpu.SemaphoreType.DMA
    scratch = dict(
        norms=vm((NS, 8, D), f32),
        aux=vm((NH, 8, R), f32),
        dirw=vm((NH, p.pairs, p.NDIR, 128), f32),
        cotb=vm((NH, RR, D), bf16),
        xbuf=vm((L + 2, NH, R, D), bf16),
        hb=vm((L, NH, R, D), bf16),
        h1b=vm((LD, NH, R, D), bf16),
        qkv=vm((L, NH, R, 3 * CW), bf16),
        cqkv=vm((LD, NH, R, 3 * CW), bf16),
        osv=vm((L, NH, R, CW), bf16),
        cosv=vm((LD, NH, R, CW), bf16),
        pre=vm((L, NH, R, FB), bf16),
        act=vm((R, FB), bf16),
        zs=vm((T, NH, RR, D), bf16),
        rstd=vm((T, NH, RR, 128), f32),
        res=vm((NH, RR, D), f32),
        gy=vm((NH, RR, D), f32),
        gag=vm((2, NH, R, D), bf16),
        gxo=vm((L, NH, RR, D), bf16),
        gmem=vm((NH, R, D), f32),
        gqkv=vm((NH, R, 3 * CW), bf16),
        gpre=vm((NH, R, FB), bf16),
        actb=vm((NH, R, FB), bf16),
        rsas=vm((2, NH, HB, D), bf16),
        rsar=vm((2, NH, HB, D), bf16),
        rsp=vm((NH, HB, D), f32),
        rsbs=vm((2, NH, K, RR, D), bf16),
        rsbr=vm((2, NH, K, RR, D), bf16),
        small=vm((NS, 16, D), f32),
        sm1=vm((TPN, NU * p.cols // 128, 16, 128), f32),
        sm1r=vm((TPN, NU * p.cols // 128, 16, 128), f32),
        sm2=vm((NU, 16, 128), f32),
        sm2r=vm((NU, 16, 128), f32),
        smo=vm((16, 128), f32),
        init_l=dma((5,)),
        init_s=dma((5,)),
        init_r=dma((5,)),
        norm_s=dma((NS,)),
        norm_r=dma((NS,)),
        a2a_s=dma((4, TPN)),
        a2a_r=dma((6, L, tz)),
        wo_s=dma((2, C)),
        ag_s=dma((nst, 6, L)),
        ag_r=dma((nst, 6, L)),
        tpa_s=dma((2, NH, K)),
        tpa_r=dma((2, NH, K)),
        tpf_s=dma((2, NH, K)),
        tpf_r=dma((2, NH, K)),
        rsa_s=dma((2, NH)),
        rsa_r=dma((2, NH)),
        rsb_s=dma((2, NH, K)),
        rsb_r=dma((2, NH, K)),
        gr_s=dma((nst, 6)),
        gr_r=dma((nst, 6)),
        credit=pltpu.SemaphoreType.REGULAR((nst, 6)),
        home_s=dma((6, tz)),
        home_r=dma((6, max(TPN, C))),
        sig_s=dma((L, NH)),
        sig_r=dma((TPN,)),
        fin_s=dma((NH,)),
        fin_r=dma((TPN,)),
        sm1_s=dma((TPN,)),
        sm1_rs=dma((TPN,)),
        sm2_s=dma((NU,)),
        sm2_rs=dma((NU,)),
        out_l=dma((L,)),
        smo_l=dma((1,)),
    )
    lagged = nst == 2
    slots = 2 if lagged else 1
    for m, block in mat_block.items():
        scratch["w%d" % m] = vm((LD if m in DECODER_MATS else L,) + two[m] + block, bf16)
        scratch["g%d" % m] = vm((slots,) + two[m] + block, bf16)
        scratch["st%d" % m] = vm((2 ** (len(two[m]) - nst),) + block, bf16)
        for j in range(1, nst + 1):
            scratch["r%d_%d" % (m, j)] = vm(two[m][j:] + block, bf16)
    in_names = ["src", "x2", "cot", "auxi", "dirwi", "normsi", "aq", "ai", "af", "ac", "woi"]
    out_names = ["out", "sig", "hq", "hi", "hf", "hc", "hwo", "smout"]
    scratch_names = list(scratch)

    def kernel(*refs):
        n = types.SimpleNamespace(**dict(zip(in_names + out_names + scratch_names, refs)))
        W = {m: getattr(n, "w%d" % m) for m in mat_block}
        A = {QKV: n.aq, FIN: n.ai, FOUT: n.af, CQKV: n.ac}
        H = {QKV: n.hq, FIN: n.hi, FOUT: n.hf, CQKV: n.hc, OUT: n.hwo, COUT: n.hc}
        G = {m: getattr(n, "g%d" % m) for m in mat_block}
        ST = {m: getattr(n, "st%d" % m) for m in mat_block}
        RB = {m: [None] + [getattr(n, "r%d_%d" % (m, j)) for j in range(1, nst + 1)] for m in mat_block}
        s, d = lax.axis_index("section"), lax.axis_index("dp")
        core, x = rm(s, 2), dv(s, 2)
        bit = [rm(dv(d, 1 << b), 2) for b in range(NB)]
        zl = bit[PAIR_BIT] if tz == 2 else 0
        k = zl * (NS // 2) + x
        r = core * K + k
        low = 1 << PAIR_BIT
        g = dv(d, 2 * low) * low + rm(d, low) if tz == 2 else d

        def place(rank, group):
            c2, k2 = dv(rank, K), rm(rank, K)
            x2, z2 = rm(k2, NS // 2), dv(k2, NS // 2)
            d2 = dv(group, low) * 2 * low + z2 * low + rm(group, low) if tz == 2 else group
            return (x2 * 2 + c2, d2)

        def with_bit(b, value):
            return d + (value - bit[b]) * (1 << b)

        def remote(src, dst, send, recv, device):
            return pltpu.make_async_remote_copy(
                src_ref=src, dst_ref=dst, send_sem=send, recv_sem=recv, device_id=device, device_id_type=MESH
            )

        def local(src, dst, sem):
            return pltpu.make_async_copy(src, dst, sem)

        def wait(ref, sem):
            pltpu.make_async_copy(ref, ref, sem).wait()

        sibling = place((1 - core) * K + k, g)

        barrier = pltpu.get_barrier_semaphore()
        total = NS * ND
        me = s * ND + d

        @pl.loop(1, total)
        def _(j):
            other = rm(me + j, total)
            pl.semaphore_signal(barrier, inc=1, device_id=(dv(other, ND), rm(other, ND)), device_id_type=MESH)

        pl.semaphore_wait(barrier, total - 1)

        own = pl.ds(mul(r, RR), RR)
        for j in range(1, NS):
            to = rm(s + j, NS)
            remote(n.normsi, n.norms.at[s], n.norm_s.at[j], n.norm_r.at[j], (to, d)).start()
        local(n.normsi, n.norms.at[s], n.norm_s.at[0]).start()
        other_rank = core * K + (1 - zl) * (NS // 2) + x
        other_rows = pl.ds(mul(other_rank, RR), RR)
        pair_dev = (s, with_bit(PAIR_BIT, 1 - zl)) if tz == 2 else None
        firsts = [
            (n.src, n.xbuf.at[0, zl], n.src, n.xbuf.at[0, zl]),
            (n.x2, n.xbuf.at[half + 1, zl], n.x2, n.xbuf.at[half + 1, zl]),
            (n.auxi, n.aux.at[zl], n.auxi, n.aux.at[zl]),
            (n.dirwi, n.dirw.at[zl], n.dirwi, n.dirw.at[zl]),
            (n.cot.at[own], n.cotb.at[zl], n.cot.at[other_rows], n.cotb.at[zl]),
        ]

        def first_start(i):
            a, b, c, e = firsts[i]
            local(a, b, n.init_l.at[i]).start()
            if tz == 2:
                remote(c, e, n.init_s.at[i], n.init_r.at[i], pair_dev).start()

        def first_wait(i):
            a, b, c, e = firsts[i]
            wait(b, n.init_l.at[i])
            if tz == 2:
                wait(e, n.init_s.at[i])
                wait(e, n.init_r.at[i])

        def wreg(m, l, fixed):
            idx = tuple(fixed.get(b, slice(None)) for b in mat_bits[m])
            return W[m].at[(l - half if m in DECODER_MATS else l,) + idx]

        mine = {b: bit[b] for b in range(NB)}

        def parts_of(m, rank):
            if m in (FIN, FOUT):
                return [((rank,), (slice(None), slice(None)))]
            return [
                ((slice(None), pl.ds(mul(part * TPN + rank, CW), CW)), (slice(None), slice(part * CW, part * CW + CW)))
                for part in range(3)
            ]

        def a2a_start(m):
            dst = wreg(m, s, mine)
            for here, there in parts_of(m, r):
                local(A[m].at[here], dst.at[there], n.a2a_r.at[m, s, zl]).start()
            for j in range(1, TPN):
                to = rm(r + j, TPN)
                for here, there in parts_of(m, to):
                    remote(A[m].at[here], dst.at[there], n.a2a_s.at[m, j], n.a2a_r.at[m, s, zl], place(to, g)).start()

        def group_bits(m, group):
            count = len(mat_bits[m])
            return tuple(rm(dv(group, 1 << (count - 1 - i)), 2) for i in range(count))

        def out_pieces(m):
            rank = dv(d, q)
            first = 3 * D if m == COUT else 0
            for c in range(C):
                group = rm(d, q) * C + c
                yield c, pl.ds(first + c * cw, cw), group, rank, (rank == r) & (group == g)

        def out_start(m, src):
            for c, span, group, rank, here in out_pieces(m):
                dst = W[m].at[(s - half if m in DECODER_MATS else s,) + group_bits(m, group)]

                @pl.when(here)
                def _():
                    local(src.at[:, span], dst, n.a2a_r.at[m, s, 0]).start()

                @pl.when(jnp.logical_not(here))
                def _():
                    remote(src.at[:, span], dst, n.wo_s.at[m - OUT, c], n.a2a_r.at[m, s, 0], place(rank, group)).start()

        def kind_layer(t):
            td = jnp.maximum(t - 2 * half, 0)
            is_enc = t < 2 * half
            tt = jnp.maximum(t, 0)
            kind = jnp.where(is_enc, 2 * rm(tt, 2), rm(td, 3))
            layer = jnp.where(is_enc, dv(tt, 2), half + dv(td, 3))
            return kind, layer

        def groups(t, fn, after_kind=None):
            valid = (t >= 0) & (t < T)
            kind, layer = kind_layer(t)
            for kd, mats in KIND_MATS.items():

                @pl.when(valid & (kind == kd))
                def _():
                    fn(kd, mats, layer)

        def ag_region(j, m, l, flip):
            fixed = {b: bit[b] for b in p.steps[j:]}
            if flip:
                fixed[p.steps[j]] = 1 - bit[p.steps[j]]
            return wreg(m, l, fixed)

        def ag_start(j, m, l):
            reg = ag_region(j, m, l, False)
            to = (s, with_bit(p.steps[j], 1 - bit[p.steps[j]]))
            remote(reg, reg, n.ag_s.at[j, m, l], n.ag_r.at[j, m, l], to).start()

        def ag_wait(j, m, l):
            if j == 0 and m in (OUT, COUT):
                wait(wreg(m, l, mine), n.a2a_r.at[m, l, 0])
            elif j == 0:
                for z in range(tz):
                    fixed = dict(mine)
                    if tz == 2:
                        fixed[PAIR_BIT] = z
                    wait(wreg(m, l, fixed), n.a2a_r.at[m, l, z])
            else:
                wait(ag_region(j - 1, m, l, True), n.ag_r.at[j - 1, m, l])

        ahead = AHEAD if nst == 2 else tuple(range(nst + 1, 0, -1))

        def feed(t):
            def fn0(kd, mats, l):
                @pl.when(l == s)
                def _():
                    for m in mats:
                        if m == OUT:
                            out_start(OUT, n.woi)
                        elif m == COUT:
                            out_start(COUT, n.ac)
                        else:
                            a2a_start(m)

            groups(t + ahead[0], fn0)
            for j in range(1, nst + 1):

                def fn(kd, mats, l, j=j):
                    for m in mats:
                        ag_wait(j - 1, m, l)
                    for m in mats:
                        ag_start(j - 1, m, l)

                groups(t + ahead[j], fn)

        def ready(t):
            def last(kd, mats, l):
                for m in mats:
                    ag_wait(nst, m, l)

            groups(t, last)

        feed(-ahead[0])
        first_start(2)
        first_start(0)

        @pl.loop(1, ahead[0])
        def _(i):
            feed(i - ahead[0])

        first_start(1)
        first_start(4)
        first_start(3)

        def tp_start(buf, h, st=0):
            mine_rows = buf.at[own]
            for j in range(1, K):
                k2 = rm(k + j, K)
                remote(mine_rows, mine_rows, n.tpa_s.at[st, h, j], n.tpa_r.at[st, h, j], place(core * K + k2, g)).start()
            remote(mine_rows, mine_rows, n.tpa_s.at[st, h, 0], n.tpa_r.at[st, h, 0], sibling).start()

        def tp_finish(buf, h, st=0):
            def rows(c2, k2):
                return buf.at[pl.ds(mul(c2 * K + k2, RR), RR)]

            for j in range(1, K):
                k2 = rm(k - j + K, K)
                ref = rows(core, k2)
                wait(ref, n.tpa_r.at[st, h, j])
                remote(ref, ref, n.tpf_s.at[st, h, j], n.tpf_r.at[st, h, j], sibling).start()
            wait(rows(1 - core, k), n.tpa_r.at[st, h, 0])
            for j in range(1, K):
                wait(rows(1 - core, rm(k - j + K, K)), n.tpf_r.at[st, h, j])
            for j in range(K):
                wait(rows(core, k), n.tpa_s.at[st, h, j])
            for j in range(1, K):
                wait(rows(core, rm(k - j + K, K)), n.tpf_s.at[st, h, j])

        def rs_start(st, h, partial):
            n.rsas[st, h] = partial(mul(1 - core, HB)).astype(bf16)
            copy = remote(n.rsas.at[st, h], n.rsar.at[st, h], n.rsa_s.at[st, h], n.rsa_r.at[st, h], sibling)
            copy.start()
            n.rsp[h] = partial(mul(core, HB))
            wait(n.rsar.at[st, h], n.rsa_r.at[st, h])
            for j in range(1, K):
                k2 = rm(k + j, K)
                rows = pl.ds(mul(k2, RR), RR)
                n.rsbs[st, h, j] = (n.rsp[h, rows] + n.rsar[st, h, rows].astype(f32)).astype(bf16)
                remote(
                    n.rsbs.at[st, h, j],
                    n.rsbr.at[st, h, j],
                    n.rsb_s.at[st, h, j],
                    n.rsb_r.at[st, h, j],
                    place(core * K + k2, g),
                ).start()
            rows = pl.ds(mul(k, RR), RR)
            n.rsp[h, rows] = n.rsp[h, rows] + n.rsar[st, h, rows].astype(f32)
            wait(n.rsas.at[st, h], n.rsa_s.at[st, h])

        def rs_finish(st, h):
            acc = n.rsp[h, pl.ds(mul(k, RR), RR)]
            for j in range(1, K):
                wait(n.rsbr.at[st, h, j], n.rsb_r.at[st, h, j])
                acc = acc + n.rsbr[st, h, j].astype(f32)
            for j in range(1, K):
                wait(n.rsbs.at[st, h, j], n.rsb_s.at[st, h, j])
            return acc

        def halves(fn):
            if NH == 1:
                fn(0)
            else:
                pl.loop(0, NH)(fn)

        def weight(m, l, lo=0, hi=None):
            hi = mat_block[m][1] if hi is None else hi
            at = (l - half if m in DECODER_MATS else l,) + (slice(None),) * (NB + 1) + (slice(lo, hi),)
            return W[m][at].reshape((-1, hi - lo))

        def out_weight(m, l, c):
            parts = [W[m][(l - half if m in DECODER_MATS else l,) + group_bits(m, a * C + c)] for a in range(q)]
            return parts[0] if q == 1 else jnp.concatenate(parts, axis=0)

        def out_product(rows, m, l):
            return jnp.concatenate([dot(rows, out_weight(m, l, c), NN) for c in range(C)], axis=1)

        def out_product_back(grad, m, l):
            acc = None
            for c in range(C):
                term = dot(grad[:, c * cw : (c + 1) * cw], out_weight(m, l, c), NT)
                acc = term if acc is None else acc + term
            return acc

        def norm_row(l, row):
            return n.norms[l][row : row + 1, :]

        def ln_forward(t, h, value, gain, bias):
            centre = value - jnp.mean(value, axis=-1, keepdims=True)
            scale = lax.rsqrt(jnp.mean(centre * centre, axis=-1, keepdims=True) + EPSILON)
            z = centre * scale
            n.zs[t, h] = z.astype(bf16)
            n.rstd[t, h] = jnp.broadcast_to(scale, (RR, 128))
            return z * gain + bias

        def ln_backward(t, h, grad, l, gain_row, bias_row):
            z = n.zs[t, h].astype(f32)
            scale = n.rstd[t, h][:, :1]
            n.small[l, gain_row : gain_row + 1, :] += jnp.sum(grad * z, axis=0, keepdims=True)
            n.small[l, bias_row : bias_row + 1, :] += jnp.sum(grad, axis=0, keepdims=True)
            gz = grad * norm_row(l, gain_row)
            return scale * (
                gz - jnp.mean(gz, axis=-1, keepdims=True) - z * jnp.mean(gz * z, axis=-1, keepdims=True)
            )

        head_width = D // HEADS
        score_scale = 1.0 / math.sqrt(head_width)

        def allowed_of(h, causal):
            rows = lax.broadcasted_iota(jnp.int32, (R, R), 0)
            cols = lax.broadcasted_iota(jnp.int32, (R, R), 1)
            ok = (dv_vec(rows) == dv_vec(cols)) & (n.aux[h][1:2] > 0.5 if causal else n.aux[h][0:1] > 0.5)
            return ok & (cols <= rows) if causal else ok

        def dv_vec(v):
            return lax.div(v, jnp.full_like(v, p.seq))

        def head_lanes(head):
            lane = lax.broadcasted_iota(jnp.int32, (1, CW), 1)
            return (lane >= head * head_width) & (lane < (head + 1) * head_width)

        def only(value, head):
            return jnp.where(head_lanes(head), value, jnp.zeros_like(value))

        def probabilities(qs, ks, allowed, head):
            scores = dot(only(qs, head), ks, NT) * score_scale
            scores = jnp.where(allowed, scores, MASKED)
            e = jnp.exp(scores - jnp.max(scores, axis=-1, keepdims=True))
            return e / jnp.sum(e, axis=-1, keepdims=True)

        def attend(qs, ks, vs, allowed):
            out = jnp.zeros((R, CW), f32)
            for head in range(p.HPR):
                probs = probabilities(qs, ks, allowed, head)
                out = out + only(dot(probs.astype(bf16), vs, NN), head)
            return out.astype(bf16)

        def attend_back(qs, ks, vs, allowed, grad):
            gq = gk = gv = jnp.zeros((R, CW), f32)
            for head in range(p.HPR):
                probs = probabilities(qs, ks, allowed, head)
                gp = dot(only(grad, head), vs, NT)
                gs = (probs * (gp - jnp.sum(gp * probs, axis=-1, keepdims=True))).astype(bf16)
                gv = gv + only(dot(probs.astype(bf16), grad, TN), head)
                gq = gq + only(dot(gs, ks, NN), head)
                gk = gk + only(dot(gs, qs, TN), head)
            return (gq * score_scale).astype(bf16), (gk * score_scale).astype(bf16), gv.astype(bf16)

        def split3(value):
            return value[:, :CW], value[:, CW : 2 * CW], value[:, 2 * CW :]

        c0, c1 = math.sqrt(2.0 / math.pi), 0.044715

        def gelu(v):
            return 0.5 * v * (1.0 + jnp.tanh(c0 * (v + c1 * (v * v * v))))

        def gelu_slope(v):
            th = jnp.tanh(c0 * (v + c1 * (v * v * v)))
            return 0.5 * (1.0 + th) + 0.5 * v * (1.0 - th * th) * (c0 * (1.0 + 3.0 * c1 * v * v))

        def rows_home(src, dst, send, recv, l, h, act):
            here = (l == s) & (h == zl)

            @pl.when(here)
            def _():
                if act == "start":
                    local(src, dst.at[own], recv.at[r]).start()

            @pl.when(jnp.logical_not(here))
            def _():
                if act == "start":
                    to = (l, with_bit(PAIR_BIT, h) if tz == 2 else d)
                    remote(src, dst.at[own], send, recv.at[r], to).start()
                else:
                    wait(src, send)

        def self_forward(l, t, xi, causal, alpha, into):
            feed(t)
            ready(t)

            def first(h):
                n.qkv[l, h] = dot(n.xbuf[xi, h], weight(QKV, l), NN).astype(bf16)
                qs, ks, vs = split3(n.qkv[l, h])
                n.osv[l, h] = attend(qs, ks, vs, allowed_of(h, causal))
                rs_start(0, h, lambda row: out_product(n.osv[l, h, pl.ds(row, HB)], OUT, l))

            def second(h):
                value = alpha * n.xbuf[xi, h, own].astype(f32) + rs_finish(0, h)
                hidden = ln_forward(t, h, value, norm_row(l, 0), norm_row(l, 2))
                n.res[h] = hidden
                into[h, own] = hidden.astype(bf16)
                tp_start(into.at[h], h)

            halves(first)
            halves(second)

        def cross_forward(l, t):
            feed(t)
            ready(t)
            ld = l - half

            def first(h):
                n.cqkv[ld, h, :, CW:] = dot(n.xbuf[half, h], weight(CQKV, l, CW), NN).astype(bf16)
                tp_finish(n.h1b.at[ld, h], h)
                n.cqkv[ld, h, :, :CW] = dot(n.h1b[ld, h], weight(CQKV, l, 0, CW), NN).astype(bf16)
                qs, ks, vs = split3(n.cqkv[ld, h])
                n.cosv[ld, h] = attend(qs, ks, vs, allowed_of(h, False))
                rs_start(0, h, lambda row: out_product(n.cosv[ld, h, pl.ds(row, HB)], COUT, l))

            def second(h):
                value = DECODER_ALPHA * n.res[h] + rs_finish(0, h)
                hidden = ln_forward(t, h, value, norm_row(l, 4), norm_row(l, 5))
                n.res[h] = hidden
                n.hb[l, h, own] = hidden.astype(bf16)
                tp_start(n.hb.at[l, h], h)

            halves(first)
            halves(second)

        def ffn_forward(l, t, xo, alpha):
            feed(t)
            ready(t)

            def first(h):
                tp_finish(n.hb.at[l, h], h)
                before = dot(n.hb[l, h], weight(FIN, l), NN)
                n.pre[l, h] = before.astype(bf16)
                n.act[...] = gelu(before).astype(bf16)
                rs_start(0, h, lambda row: dot(n.act[pl.ds(row, HB)], weight(FOUT, l), NN))

            def second(h):
                value = alpha * n.res[h] + rs_finish(0, h)
                result = ln_forward(t, h, value, norm_row(l, 1), norm_row(l, 3))
                n.xbuf[xo, h, own] = result.astype(bf16)

                @pl.when(l < L - 1)
                def _():
                    tp_start(n.xbuf.at[xo, h], h, 1)

                @pl.when(l == L - 1)
                def _():
                    rows_home(n.xbuf.at[xo, h, own], n.out, n.fin_s.at[h], n.fin_r, L - 1, h, "start")

            def third(h):
                tp_finish(n.xbuf.at[xo, h], h, 1)

            halves(first)
            halves(second)

            @pl.when(l < L - 1)
            def _():
                halves(third)

                @pl.when(s == l)
                def _():
                    local(n.xbuf.at[xo, zl], n.out, n.out_l.at[0]).start()

        for i in (2, 0):
            first_wait(i)
        for j in range(1, NS):
            wait(n.norms.at[rm(s - j + NS, NS)], n.norm_r.at[j])
        wait(n.norms.at[s], n.norm_s.at[0])
        n.small[...] = jnp.zeros_like(n.small)
        n.gmem[...] = jnp.zeros_like(n.gmem)

        @pl.loop(0, half)
        def _(l):
            self_forward(l, 2 * l, l, False, ENCODER_ALPHA, n.hb.at[l])
            ffn_forward(l, 2 * l + 1, l + 1, ENCODER_ALPHA)

        for i in (1, 3, 4):
            first_wait(i)

        @pl.loop(half, L)
        def _(l):
            t = 2 * half + 3 * (l - half)
            self_forward(l, t, l + 1, True, DECODER_ALPHA, n.h1b.at[l - half])
            cross_forward(l, t + 1)
            ffn_forward(l, t + 2, l + 2, DECODER_ALPHA)

        def gbuf(m, l):
            return G[m].at[rm(l, slots)]

        def gregion(m, l, fixed):
            return gbuf(m, l).at[tuple(fixed.get(b, slice(None)) for b in mat_bits[m])]

        def partner(j):
            b = back_steps[j - 1]
            return (s, with_bit(b, 1 - bit[b]))

        def gr_start(j, m, l):
            @pl.when(l != L - 1)
            def _():
                pl.semaphore_wait(n.credit.at[j - 1, m], 1)

            fixed = {b: bit[b] for b in back_steps[: j - 1]}
            fixed[back_steps[j - 1]] = 1 - bit[back_steps[j - 1]]
            remote(gregion(m, l, fixed), RB[m][j], n.gr_s.at[j - 1, m], n.gr_r.at[j - 1, m], partner(j)).start()

        def blocks_of(count):
            return [
                tuple((i >> b) & 1 for b in reversed(range(count))) for i in range(1 << count)
            ]

        def gr_finish(j, m, l):
            wait(RB[m][j], n.gr_r.at[j - 1, m])
            mine_part = gregion(m, l, {b: bit[b] for b in back_steps[:j]})
            for idx in blocks_of(len(mat_bits[m]) - j):
                value = mine_part[idx].astype(f32) + RB[m][j][idx].astype(f32)
                if j == nst:
                    ST[m][idx if idx else 0] = value.astype(bf16)
                else:
                    mine_part[idx] = value.astype(bf16)
            wait(RB[m][j], n.gr_s.at[j - 1, m])

            @pl.when(l != (half if m in DECODER_MATS else 0))
            def _():
                pl.semaphore_signal(n.credit.at[j - 1, m], inc=1, device_id=partner(j), device_id_type=MESH)

            if j < nst:
                gr_start(j + 1, m, l)
            else:
                for z in range(ST[m].shape[0]):
                    home(m, l, z, "start")

        def homes_wait(m, l):
            for z in range(ST[m].shape[0]):
                home(m, l, z, "wait")

        def home(m, l, z, act):
            src = ST[m].at[z]
            if m in (OUT, COUT):
                piece = rm(g, C)
                to = (l, r * q + dv(g, C))
                here = (l == s) & (to[1] == d)
                first = 3 * D if m == COUT else 0
                copies = [(src, H[m].at[:, pl.ds(pl.multiple_of(first + piece * cw, cw), cw)])]
                slot = piece
            else:
                to = (l, with_bit(PAIR_BIT, z) if tz == 2 else d)
                here = (l == s) & (zl == z) if tz == 2 else l == s
                copies = [(src.at[b], H[m].at[a]) for a, b in parts_of(m, r)]
                slot = r
            if act == "wait":
                wait(src, n.home_s.at[m, z])
                return

            @pl.when(here)
            def _():
                for a, b in copies:
                    local(a, b, n.home_s.at[m, z]).start()

            @pl.when(jnp.logical_not(here))
            def _():
                for a, b in copies:
                    remote(a, b, n.home_s.at[m, z], n.home_r.at[m, slot], to).start()

        def homes_wait(m, l):
            for z in range(ST[m].shape[0]):
                home(m, l, z, "wait")

        def process(u):
            if not lagged:
                return

            def old(kd, mats, l):
                for m in mats:
                    homes_wait(m, l)

            groups(T - 1 - (u - BEHIND[nst - 1] - 1), old)
            for j in range(1, nst + 1):

                def fn(kd, mats, l, j=j):
                    for m in mats:
                        gr_finish(j, m, l)

                groups(T - 1 - (u - BEHIND[j - 1]), fn)

        def send_grad(m, l):
            gr_start(1, m, l)
            if not lagged:
                for j in range(1, nst + 1):
                    gr_finish(j, m, l)
                homes_wait(m, l)

        def weight_grad(m, l, lefts, rights):
            rows, cols = mat_block[m]
            count = max(1, 128 // rows)
            tile = rows * count

            @pl.loop(0, ND // count)
            def _(i):
                span = pl.ds(mul(i, tile), tile)
                parts = []
                for left, right in zip(lefts, rights):
                    acc = None
                    for h in range(NH):
                        term = dot(left[h][:, span], right[h][...], TN)
                        acc = term if acc is None else acc + term
                    parts.append(acc)
                value = parts[0] if len(parts) == 1 else jnp.concatenate(parts, axis=1)
                value = value.astype(bf16)
                for e in range(count):
                    at = i * count + e
                    idx = tuple(rm(dv(at, 1 << b), 2) for b in reversed(range(NB)))
                    gbuf(m, l)[idx] = value[e * rows : (e + 1) * rows]

        def out_grad(m, l, left, right):
            for c in range(C):
                acc = None
                for h in range(NH):
                    term = dot(left[h][...], right[h][:, c * cw : (c + 1) * cw], TN)
                    acc = term if acc is None else acc + term
                acc = acc.astype(bf16)
                for a in range(q):
                    gbuf(m, l)[group_bits(m, a * C + c)] = acc[a * p.rb : (a + 1) * p.rb]

        def each(ref):
            return [ref.at[h] for h in range(NH)]

        def branch_grad(t, l, u, gain_row, bias_row):
            gag = n.gag.at[rm(u, 2)]

            def fn(h):
                grad = ln_backward(t, h, n.gy[h], l, gain_row, bias_row)
                n.res[h] = grad
                gag[h, own] = grad.astype(bf16)
                tp_start(gag.at[h], h)

            halves(fn)
            return gag

        def ffn_backward(l, t, u, alpha):
            gag = branch_grad(t, l, u, 1, 3)

            def first(h):
                tp_finish(gag.at[h], h)
                before = n.pre[l, h].astype(f32)
                gact = dot(gag[h], weight(FOUT, l), NT)
                n.gpre[h] = (gact * gelu_slope(before)).astype(bf16)
                rs_start(0, h, lambda row: dot(n.gpre[h, pl.ds(row, HB)], weight(FIN, l), NT))
                n.actb[h] = gelu(before).astype(bf16)

            halves(first)
            weight_grad(FOUT, l, [each(n.actb)], [each(gag)])
            process(u)
            send_grad(FOUT, l)
            weight_grad(FIN, l, [each(n.hb.at[l])], [each(n.gpre)])
            send_grad(FIN, l)

            def second(h):
                n.gy[h] = alpha * n.res[h] + rs_finish(0, h)

            halves(second)

        def cross_backward(l, t, u):
            gag = branch_grad(t, l, u, 4, 5)
            ld = l - half

            def first(h):
                tp_finish(gag.at[h], h)
                grad = out_product_back(gag.at[h], COUT, l).astype(bf16)
                qs, ks, vs = split3(n.cqkv[ld, h])
                gq, gk, gv = attend_back(qs, ks, vs, allowed_of(h, False), grad)
                n.gqkv[h, :, :CW] = gq
                n.gqkv[h, :, CW : 2 * CW] = gk
                n.gqkv[h, :, 2 * CW :] = gv
                rs_start(
                    0, h, lambda row: dot(n.gqkv[h, pl.ds(row, HB), :CW], weight(CQKV, l, 0, CW), NT)
                )
                n.gmem[h] += dot(n.gqkv[h, :, CW:], weight(CQKV, l, CW), NT)

            halves(first)
            out_grad(COUT, l, each(n.cosv.at[ld]), each(gag))
            process(u)
            send_grad(COUT, l)
            weight_grad(
                CQKV,
                l,
                [each(n.h1b.at[ld]), each(n.xbuf.at[half])],
                [
                    [n.gqkv.at[h, :, pl.ds(0, CW)] for h in range(NH)],
                    [n.gqkv.at[h, :, pl.ds(CW, 2 * CW)] for h in range(NH)],
                ],
            )
            send_grad(CQKV, l)

            def second(h):
                n.gy[h] = DECODER_ALPHA * n.res[h] + rs_finish(0, h)

            halves(second)

        def sig_copy(l, h, act):
            rows_home(n.gxo.at[l, h], n.sig, n.sig_s.at[l, h], n.sig_r, l, h, act)

        def self_backward(l, t, u, xi, causal, alpha):
            gag = branch_grad(t, l, u, 0, 2)

            def first(h):
                tp_finish(gag.at[h], h)
                grad = out_product_back(gag.at[h], OUT, l).astype(bf16)
                qs, ks, vs = split3(n.qkv[l, h])
                gq, gk, gv = attend_back(qs, ks, vs, allowed_of(h, causal), grad)
                n.gqkv[h, :, :CW] = gq
                n.gqkv[h, :, CW : 2 * CW] = gk
                n.gqkv[h, :, 2 * CW :] = gv
                rs_start(0, h, lambda row: dot(n.gqkv[h, pl.ds(row, HB)], weight(QKV, l), NT))

            halves(first)
            out_grad(OUT, l, each(n.osv.at[l]), each(gag))
            process(u)
            send_grad(OUT, l)
            weight_grad(QKV, l, [each(n.xbuf.at[xi])], [each(n.gqkv)])
            send_grad(QKV, l)

            def second(h):
                grad = (alpha * n.res[h] + rs_finish(0, h)).astype(bf16)
                n.gxo[l, h] = grad
                n.gy[h] = grad.astype(f32)
                sig_copy(l, h, "start")

            halves(second)

        def seed(h):
            n.gy[h] = n.cotb[h].astype(f32)

        halves(seed)

        @pl.loop(0, LD)
        def _(i):
            l = L - 1 - i
            t = 2 * half + 3 * (l - half)
            ffn_backward(l, t + 2, 3 * i, DECODER_ALPHA)
            cross_backward(l, t + 1, 3 * i + 1)
            self_backward(l, t, 3 * i + 2, l + 1, True, DECODER_ALPHA)

        def directions(h):
            column = n.dirw[h, dv(r * RR, p.seq)][:, :1]
            rows = column * jnp.sum(n.gy[h], axis=0, keepdims=True)
            for sec in range(NS):
                lo = sec * p.dir_rows
                n.small[sec, 8 : 8 + p.dir_rows, :] += rows[lo : lo + p.dir_rows]

        halves(directions)

        def memory_first(h):
            rs_start(1, h, lambda row: n.gmem[h, pl.ds(row, HB)])

        def memory_second(h):
            n.gy[h] = rs_finish(1, h).astype(bf16).astype(f32)

        halves(memory_first)
        halves(memory_second)

        @pl.loop(0, half)
        def _(i):
            l = half - 1 - i
            u = 3 * LD + 2 * i
            ffn_backward(l, 2 * l + 1, u, ENCODER_ALPHA)
            self_backward(l, 2 * l, u + 1, l, False, ENCODER_ALPHA)

        process(T)

        for rank in range(TPN):
            for g2 in range(NU):
                sec, d2 = place(rank, g2)
                lo = d2 * p.cols
                tile, lane = divmod(g2 * p.cols, 128)
                n.sm1[rank, tile, :, lane : lane + p.cols] = n.small[sec, :, lo : lo + p.cols]
        for j in range(1, TPN):
            to = rm(r + j, TPN)
            remote(n.sm1.at[to], n.sm1r.at[j], n.sm1_s.at[j], n.sm1_rs.at[j], place(to, g)).start()

        if lagged:

            @pl.loop(1, BEHIND[nst - 1] + 1)
            def _(i):
                process(T + i)

        total_small = n.sm1[r]
        for j in range(1, TPN):
            wait(n.sm1r.at[j], n.sm1_rs.at[j])
            total_small = total_small + n.sm1r[j]
        for g2 in range(NU):
            tile, lane = divmod(g2 * p.cols, 128)
            n.sm2[g2, :, : p.cols] = total_small[tile, :, lane : lane + p.cols]
        for j in range(1, NU):
            to = rm(g + j, NU)
            remote(n.sm2.at[to], n.sm2r.at[j], n.sm2_s.at[j], n.sm2_rs.at[j], place(r, to)).start()
        mine_small = n.sm2[g]
        for j in range(1, NU):
            wait(n.sm2r.at[j], n.sm2_rs.at[j])
            mine_small = mine_small + n.sm2r[j]
        n.smo[...] = mine_small
        local(n.smo, n.smout, n.smo_l.at[0]).start()
        wait(n.smo, n.smo_l.at[0])

        def home_wait(m):
            for j in range(1, TPN):
                rank = rm(r + j, TPN)
                wait(ST[m].at[0], n.home_r.at[m, rank])

        def home_wait_out(m):
            for c, span, group, rank, here in out_pieces(m):

                @pl.when(jnp.logical_not(here))
                def _():
                    wait(H[m].at[:, span], n.home_r.at[m, c])

        for m in (QKV, FIN, FOUT):
            home_wait(m)
        home_wait_out(OUT)

        @pl.when(s >= half)
        def _():
            home_wait(CQKV)
            home_wait_out(COUT)

        for rank in range(TPN):
            wait(n.sig.at[pl.ds(rank * RR, RR)], n.sig_r.at[rank])
        @pl.when(s < L - 1)
        def _():
            wait(n.out, n.out_l.at[0])

        @pl.when(s == L - 1)
        def _():
            for rank in range(TPN):
                wait(n.out.at[pl.ds(rank * RR, RR)], n.fin_r.at[rank])

        for h in range(NH):
            rows_home(n.xbuf.at[L + 1, h, own], n.out, n.fin_s.at[h], n.fin_r, L - 1, h, "wait")
        for l in range(L):
            for h in range(NH):
                sig_copy(l, h, "wait")
        for j in range(1, TPN):
            wait(n.sm1.at[0], n.sm1_s.at[j])
        for j in range(1, NU):
            wait(n.sm2.at[0], n.sm2_s.at[j])
        for j in range(1, NS):
            wait(n.norms.at[0], n.norm_s.at[j])
        for j in range(1, TPN):
            for m in (QKV, FIN, FOUT):
                wait(ST[m].at[0], n.a2a_s.at[m, j])

        @pl.when(s >= half)
        def _():
            for j in range(1, TPN):
                wait(ST[CQKV].at[0], n.a2a_s.at[CQKV, j])

        for m in (OUT, COUT):
            for c, span, group, rank, here in out_pieces(m):
                sends = jnp.logical_not(here) if m == OUT else jnp.logical_not(here) & (s >= half)

                @pl.when(sends)
                def _():
                    wait(ST[m].at[0], n.wo_s.at[m - OUT, c])

        @pl.loop(0, L)
        def _(l):
            for j in range(nst):
                for m in mat_block:
                    if m not in DECODER_MATS:
                        wait(ag_region(j, m, l, False), n.ag_s.at[j, m, l])

                @pl.when(l >= half)
                def _():
                    for m in DECODER_MATS:
                        wait(ag_region(j, m, l, False), n.ag_s.at[j, m, l])

    def sd(*shape, dtype=bf16):
        return jax.ShapeDtypeStruct(shape, dtype)

    def blocks(m, lead):
        return sd(lead, *mat_block[m])

    outs = [
        sd(R, D),
        sd(R, D),
        sd(p.rb, 3 * D),
        blocks(FIN, TPN),
        blocks(FOUT, TPN),
        sd(p.rb, 4 * D),
        sd(p.rb, D),
        sd(16, 128, dtype=f32),
    ]
    anywhere = pl.BlockSpec(memory_space=pl.ANY)
    return pl.pallas_call(
        kernel,
        out_shape=outs,
        in_specs=[anywhere] * len(in_names),
        out_specs=[anywhere] * len(out_names),
        scratch_shapes=list(scratch.values()),
        compiler_params=pltpu.CompilerParams(
            collective_id=0, has_side_effects=True, vmem_limit_bytes=64 * 1024 * 1024 - 64 * 1024
        ),
    )


def solution(mesh):
    def body(
        source,
        target,
        directions,
        source_lengths,
        target_lengths,
        attn_in,
        attn_out,
        ffn_in,
        ffn_out,
        cross_weight,
        norm_gain,
        norm_bias,
        cross_norm,
        dir_table,
        cotangent,
    ):
        pairs, seq, width = source.shape
        p = make_plan(
            mesh.shape["section"], mesh.shape["dp"], pairs, seq, width, ffn_in.shape[2], dir_table.shape[0]
        )
        section = lax.axis_index("section")
        routing = (directions[:, None] == jnp.arange(p.NDIR)[None, :]).astype(f32)
        rows = jnp.dot(routing, dir_table, precision=lax.Precision.HIGHEST)
        x2 = (target.astype(f32) + rows[:, None, :]).astype(bf16).reshape(p.R, width)
        positions = jnp.arange(seq)
        valid = [(positions[None, :] < lens[:, None]).astype(f32).reshape(1, p.R) for lens in (source_lengths, target_lengths)]
        aux = jnp.concatenate(valid + [jnp.zeros((6, p.R), f32)], axis=0)
        dirw = jnp.broadcast_to(routing[:, :, None], (pairs, p.NDIR, 128))
        norms = jnp.concatenate(
            (norm_gain[0], norm_bias[0], cross_norm[0], jnp.zeros((2, width), bf16)), axis=0
        ).astype(f32)
        ai = ffn_in[0].reshape(p.rb, p.ND, p.TPN, p.fb).transpose(2, 0, 1, 3).reshape(p.TPN, p.rb, p.FB)
        af = ffn_out[0].reshape(p.TPN, p.fb, width)
        out, sig, hq, hi, hf, hc, hwo, small = build(p)(
            source.reshape(p.R, width),
            x2,
            cotangent.reshape(p.R, width),
            aux,
            dirw,
            norms,
            attn_in[0],
            ai,
            af,
            cross_weight[0],
            attn_out[0],
        )
        decoder = section >= p.half

        g_in = hi.reshape(p.TPN, p.rb, p.ND, p.fb).transpose(1, 2, 0, 3).reshape(1, p.rb, p.FF).astype(f32)
        g_out = hf.reshape(1, p.TPN * p.fb, width).astype(f32)
        g_wo = hwo.astype(f32)[None]
        g_cross = jnp.where(decoder, hc.astype(f32), jnp.zeros(hc.shape, f32))[None]
        small = small[:, : p.cols]
        return (
            out.reshape(1, pairs, seq, width),
            sig.reshape(1, pairs, seq, width),
            hq.astype(f32)[None],
            g_wo,
            g_in,
            g_out,
            g_cross,
            small[None, 0:2],
            small[None, 2:4],
            small[None, 4:6],
            small[8 : 8 + p.dir_rows],
        )

    sharded = P("section", "dp", None)
    return jax.shard_map(
        body,
        mesh=mesh,
        in_specs=(
            P("dp", None, None),
            P("dp", None, None),
            P("dp"),
            P("dp"),
            P("dp"),
            sharded,
            sharded,
            sharded,
            sharded,
            sharded,
            P("section", None, None),
            P("section", None, None),
            P("section", None, None),
            P(),
            P("dp", None, None),
        ),
        out_specs=(
            P("section", "dp", None, None),
            P("section", "dp", None, None),
            sharded,
            sharded,
            sharded,
            sharded,
            sharded,
            P("section", None, "dp"),
            P("section", None, "dp"),
            P("section", None, "dp"),
            P("section", "dp"),
        ),
        check_vma=False,
    )
```

```python
import math
import types

import jax
import jax.numpy as jnp
from jax import lax
from jax.experimental import pallas as pl
from jax.experimental.pallas import tpu as pltpu
from jax.sharding import PartitionSpec as P

HEADS = 16
GROUP = 8
AHEAD = (5, 4, 2)
BEHIND = (2, 3)
PAIR_BIT = 0
ENCODER_ALPHA = 3.42
DECODER_ALPHA = 4.16
MASKED = -1000000000.0
EPSILON = 1e-05
MESH = pl.DeviceIdType.MESH
f32, bf16 = jnp.float32, jnp.bfloat16
NN, NT, TN = (((1,), (0,)), ((), ())), (((1,), (1,)), ((), ())), (((0,), (0,)), ((), ()))
ATTN, CROSS, FFN = 0, 1, 2
QKV, FIN, FOUT, CQKV, OUT, COUT = range(6)
KIND_MATS = {ATTN: (QKV, OUT), CROSS: (CQKV, COUT), FFN: (FOUT, FIN)}
DECODER_MATS = (CQKV, COUT)


def dot(a, b, dims):
    return lax.dot_general(a, b, dims, preferred_element_type=f32)


def dv(a, b):
    return a // b if isinstance(a, int) else lax.div(a, jnp.int32(b))


def rm(a, b):
    return a % b if isinstance(a, int) else lax.rem(a, jnp.int32(b))


def mul(a, b):
    return pl.multiple_of(a * b, b)


def make_plan(sections, dp_count, pairs, seq, width, ff, directions):
    p = types.SimpleNamespace()
    p.NS, p.ND, p.L, p.half = sections, dp_count, sections, sections // 2
    p.pairs, p.seq, p.D, p.FF, p.R = pairs, seq, width, ff, pairs * seq
    p.tz = 2 if sections < GROUP and dp_count >= 4 else 1
    p.TPN = sections * p.tz
    p.K = p.TPN // 2
    p.RR = p.R // p.TPN
    p.CW = width // p.TPN
    p.HPR = HEADS // p.TPN
    p.FB = ff // p.TPN
    p.rb = width // dp_count
    p.fb = ff // dp_count // p.TPN
    p.q = dp_count // p.TPN
    p.NU = dp_count // p.tz
    p.C = p.NU // p.q
    p.cw = width // p.C
    p.NB = dp_count.bit_length() - 1
    if p.tz == 2:
        p.steps = [b for b in reversed(range(p.NB)) if b != PAIR_BIT]
    else:
        p.steps = list(range(p.NB))
    p.nst = len(p.steps)
    p.T = 2 * p.half + 3 * (p.L - p.half)
    p.NDIR = directions
    p.dir_rows = directions // sections
    p.cols = width // dp_count
    return p


def build(p):
    NS, ND, L, half, TPN, K, RR, R, D = p.NS, p.ND, p.L, p.half, p.TPN, p.K, p.RR, p.R, p.D
    CW, FB, NU, NB, nst, T, tz, q = p.CW, p.FB, p.NU, p.NB, p.nst, p.T, p.tz, p.q
    NH, LD = tz, p.L - p.half
    HB = K * RR
    C, cw = p.C, p.cw
    mat_block = {
        QKV: (p.rb, 3 * CW),
        FIN: (p.rb, FB),
        FOUT: (p.fb, D),
        CQKV: (p.rb, 3 * CW),
        OUT: (p.rb, cw),
        COUT: (p.rb, cw),
    }
    all_bits = list(reversed(range(NB)))
    mat_bits = {m: [b for b in all_bits if b in p.steps] if m in (OUT, COUT) else all_bits for m in mat_block}
    two = {m: (2,) * len(mat_bits[m]) for m in mat_block}
    back_steps = p.steps[::-1]

    vm, dma = pltpu.VMEM, pltpu.SemaphoreType.DMA
    scratch = dict(
        norms=vm((NS, 8, D), f32),
        aux=vm((NH, 8, R), f32),
        dirw=vm((NH, p.pairs, p.NDIR, 128), f32),
        cotb=vm((NH, RR, D), bf16),
        xbuf=vm((L + 2, NH, R, D), bf16),
        hb=vm((L, NH, R, D), bf16),
        h1b=vm((LD, NH, R, D), bf16),
        qkv=vm((L, NH, R, 3 * CW), bf16),
        cqkv=vm((LD, NH, R, 3 * CW), bf16),
        osv=vm((L, NH, R, CW), bf16),
        cosv=vm((LD, NH, R, CW), bf16),
        pre=vm((L, NH, R, FB), bf16),
        zs=vm((T, NH, RR, D), bf16),
        rstd=vm((T, NH, RR, 128), f32),
        res=vm((NH, RR, D), f32),
        gy=vm((NH, RR, D), f32),
        gag=vm((2, NH, R, D), bf16),
        gxo=vm((L, NH, RR, D), bf16),
        gmem=vm((NH, R, D), f32),
        gqkv=vm((NH, R, 3 * CW), bf16),
        gpre=vm((NH, R, FB), bf16),
        actb=vm((NH, R, FB), bf16),
        rsas=vm((2, NH, HB, D), bf16),
        rsar=vm((2, NH, HB, D), bf16),
        rsp=vm((NH, HB, D), f32),
        rsbs=vm((2, NH, K, RR, D), bf16),
        rsbr=vm((2, NH, K, RR, D), bf16),
        small=vm((NS, 16, D), f32),
        sm1=vm((TPN, NU * p.cols // 128, 16, 128), f32),
        sm1r=vm((TPN, NU * p.cols // 128, 16, 128), f32),
        sm2=vm((NU, 16, 128), f32),
        sm2r=vm((NU, 16, 128), f32),
        smo=vm((16, 128), f32),
        init_l=dma((5,)),
        init_s=dma((5,)),
        init_r=dma((5,)),
        norm_s=dma((NS,)),
        norm_r=dma((NS,)),
        a2a_s=dma((4, TPN)),
        a2a_r=dma((6, L, tz)),
        wo_s=dma((2, C)),
        ag_s=dma((nst, 6, L)),
        ag_r=dma((nst, 6, L)),
        tpa_s=dma((2, NH, K)),
        tpa_r=dma((2, NH, K)),
        tpf_s=dma((2, NH, K)),
        tpf_r=dma((2, NH, K)),
        rsa_s=dma((2, NH)),
        rsa_r=dma((2, NH)),
        rsb_s=dma((2, NH, K)),
        rsb_r=dma((2, NH, K)),
        gr_s=dma((nst, 6)),
        gr_r=dma((nst, 6)),
        credit=pltpu.SemaphoreType.REGULAR((nst, 6)),
        home_s=dma((6, tz)),
        home_r=dma((6, max(TPN, C))),
        sig_s=dma((L, NH)),
        sig_r=dma((TPN,)),
        fin_s=dma((NH,)),
        fin_r=dma((TPN,)),
        sm1_s=dma((TPN,)),
        sm1_rs=dma((TPN,)),
        sm2_s=dma((NU,)),
        sm2_rs=dma((NU,)),
        out_l=dma((L,)),
        smo_l=dma((1,)),
    )
    lagged = nst == 2
    slots = 2 if lagged else 1
    for m, block in mat_block.items():
        scratch["w%d" % m] = vm((LD if m in DECODER_MATS else L,) + two[m] + block, bf16)
        scratch["g%d" % m] = vm((slots,) + two[m] + block, bf16)
        scratch["st%d" % m] = vm((2 ** (len(two[m]) - nst),) + block, bf16)
        for j in range(1, nst + 1):
            scratch["r%d_%d" % (m, j)] = vm(two[m][j:] + block, bf16)
    in_names = ["src", "x2", "cot", "auxi", "dirwi", "normsi", "aq", "ai", "af", "ac", "woi"]
    out_names = ["out", "sig", "hq", "hi", "hf", "hc", "hwo", "smout"]
    scratch_names = list(scratch)

    def kernel(*refs):
        n = types.SimpleNamespace(**dict(zip(in_names + out_names + scratch_names, refs)))
        W = {m: getattr(n, "w%d" % m) for m in mat_block}
        A = {QKV: n.aq, FIN: n.ai, FOUT: n.af, CQKV: n.ac}
        H = {QKV: n.hq, FIN: n.hi, FOUT: n.hf, CQKV: n.hc, OUT: n.hwo, COUT: n.hc}
        G = {m: getattr(n, "g%d" % m) for m in mat_block}
        ST = {m: getattr(n, "st%d" % m) for m in mat_block}
        RB = {m: [None] + [getattr(n, "r%d_%d" % (m, j)) for j in range(1, nst + 1)] for m in mat_block}
        s, d = lax.axis_index("section"), lax.axis_index("dp")
        core, x = rm(s, 2), dv(s, 2)
        bit = [rm(dv(d, 1 << b), 2) for b in range(NB)]
        zl = bit[PAIR_BIT] if tz == 2 else 0
        k = zl * (NS // 2) + x
        r = core * K + k
        low = 1 << PAIR_BIT
        g = dv(d, 2 * low) * low + rm(d, low) if tz == 2 else d

        def place(rank, group):
            c2, k2 = dv(rank, K), rm(rank, K)
            x2, z2 = rm(k2, NS // 2), dv(k2, NS // 2)
            d2 = dv(group, low) * 2 * low + z2 * low + rm(group, low) if tz == 2 else group
            return (x2 * 2 + c2, d2)

        def with_bit(b, value):
            return d + (value - bit[b]) * (1 << b)

        def remote(src, dst, send, recv, device):
            return pltpu.make_async_remote_copy(
                src_ref=src, dst_ref=dst, send_sem=send, recv_sem=recv, device_id=device, device_id_type=MESH
            )

        def local(src, dst, sem):
            return pltpu.make_async_copy(src, dst, sem)

        def wait(ref, sem):
            pltpu.make_async_copy(ref, ref, sem).wait()

        sibling = place((1 - core) * K + k, g)

        barrier = pltpu.get_barrier_semaphore()
        total = NS * ND
        me = s * ND + d

        @pl.loop(1, total)
        def _(j):
            other = rm(me + j, total)
            pl.semaphore_signal(barrier, inc=1, device_id=(dv(other, ND), rm(other, ND)), device_id_type=MESH)

        pl.semaphore_wait(barrier, total - 1)

        own = pl.ds(mul(r, RR), RR)
        for j in range(1, NS):
            to = rm(s + j, NS)
            remote(n.normsi, n.norms.at[s], n.norm_s.at[j], n.norm_r.at[j], (to, d)).start()
        local(n.normsi, n.norms.at[s], n.norm_s.at[0]).start()
        other_rank = core * K + (1 - zl) * (NS // 2) + x
        other_rows = pl.ds(mul(other_rank, RR), RR)
        pair_dev = (s, with_bit(PAIR_BIT, 1 - zl)) if tz == 2 else None
        firsts = [
            (n.src, n.xbuf.at[0, zl], n.src, n.xbuf.at[0, zl]),
            (n.x2, n.xbuf.at[half + 1, zl], n.x2, n.xbuf.at[half + 1, zl]),
            (n.auxi, n.aux.at[zl], n.auxi, n.aux.at[zl]),
            (n.dirwi, n.dirw.at[zl], n.dirwi, n.dirw.at[zl]),
            (n.cot.at[own], n.cotb.at[zl], n.cot.at[other_rows], n.cotb.at[zl]),
        ]

        def first_start(i):
            a, b, c, e = firsts[i]
            local(a, b, n.init_l.at[i]).start()
            if tz == 2:
                remote(c, e, n.init_s.at[i], n.init_r.at[i], pair_dev).start()

        def first_wait(i):
            a, b, c, e = firsts[i]
            wait(b, n.init_l.at[i])
            if tz == 2:
                wait(e, n.init_s.at[i])
                wait(e, n.init_r.at[i])

        def wreg(m, l, fixed):
            idx = tuple(fixed.get(b, slice(None)) for b in mat_bits[m])
            return W[m].at[(l - half if m in DECODER_MATS else l,) + idx]

        mine = {b: bit[b] for b in range(NB)}

        def parts_of(m, rank):
            if m in (FIN, FOUT):
                return [((rank,), (slice(None), slice(None)))]
            return [
                ((slice(None), pl.ds(mul(part * TPN + rank, CW), CW)), (slice(None), slice(part * CW, part * CW + CW)))
                for part in range(3)
            ]

        def a2a_start(m):
            dst = wreg(m, s, mine)
            for here, there in parts_of(m, r):
                local(A[m].at[here], dst.at[there], n.a2a_r.at[m, s, zl]).start()
            for j in range(1, TPN):
                to = rm(r + j, TPN)
                for here, there in parts_of(m, to):
                    remote(A[m].at[here], dst.at[there], n.a2a_s.at[m, j], n.a2a_r.at[m, s, zl], place(to, g)).start()

        def group_bits(m, group):
            count = len(mat_bits[m])
            return tuple(rm(dv(group, 1 << (count - 1 - i)), 2) for i in range(count))

        def out_pieces(m):
            rank = dv(d, q)
            first = 3 * D if m == COUT else 0
            for c in range(C):
                group = rm(d, q) * C + c
                yield c, pl.ds(first + c * cw, cw), group, rank, (rank == r) & (group == g)

        def out_start(m, src):
            for c, span, group, rank, here in out_pieces(m):
                dst = W[m].at[(s - half if m in DECODER_MATS else s,) + group_bits(m, group)]

                @pl.when(here)
                def _():
                    local(src.at[:, span], dst, n.a2a_r.at[m, s, 0]).start()

                @pl.when(jnp.logical_not(here))
                def _():
                    remote(src.at[:, span], dst, n.wo_s.at[m - OUT, c], n.a2a_r.at[m, s, 0], place(rank, group)).start()

        def kind_layer(t):
            td = jnp.maximum(t - 2 * half, 0)
            is_enc = t < 2 * half
            tt = jnp.maximum(t, 0)
            kind = jnp.where(is_enc, 2 * rm(tt, 2), rm(td, 3))
            layer = jnp.where(is_enc, dv(tt, 2), half + dv(td, 3))
            return kind, layer

        def groups(t, fn, after_kind=None):
            valid = (t >= 0) & (t < T)
            kind, layer = kind_layer(t)
            for kd, mats in KIND_MATS.items():

                @pl.when(valid & (kind == kd))
                def _():
                    fn(kd, mats, layer)

        def ag_region(j, m, l, flip):
            fixed = {b: bit[b] for b in p.steps[j:]}
            if flip:
                fixed[p.steps[j]] = 1 - bit[p.steps[j]]
            return wreg(m, l, fixed)

        def ag_start(j, m, l):
            reg = ag_region(j, m, l, False)
            to = (s, with_bit(p.steps[j], 1 - bit[p.steps[j]]))
            remote(reg, reg, n.ag_s.at[j, m, l], n.ag_r.at[j, m, l], to).start()

        def ag_wait(j, m, l):
            if j == 0 and m in (OUT, COUT):
                wait(wreg(m, l, mine), n.a2a_r.at[m, l, 0])
            elif j == 0:
                for z in range(tz):
                    fixed = dict(mine)
                    if tz == 2:
                        fixed[PAIR_BIT] = z
                    wait(wreg(m, l, fixed), n.a2a_r.at[m, l, z])
            else:
                wait(ag_region(j - 1, m, l, True), n.ag_r.at[j - 1, m, l])

        ahead = AHEAD if nst == 2 else tuple(range(nst + 1, 0, -1))

        def feed(t):
            def fn0(kd, mats, l):
                @pl.when(l == s)
                def _():
                    for m in mats:
                        if m == OUT:
                            out_start(OUT, n.woi)
                        elif m == COUT:
                            out_start(COUT, n.ac)
                        else:
                            a2a_start(m)

            groups(t + ahead[0], fn0)
            for j in range(1, nst + 1):

                def fn(kd, mats, l, j=j):
                    for m in reversed(mats):
                        ag_wait(j - 1, m, l)
                        ag_start(j - 1, m, l)

                groups(t + ahead[j], fn)

        def ready(l, *mats):
            for m in mats:
                ag_wait(nst, m, l)

        feed(-ahead[0])
        first_start(2)
        first_start(0)

        @pl.loop(1, ahead[0])
        def _(i):
            feed(i - ahead[0])

        first_start(1)
        first_start(4)
        first_start(3)

        def tp_start(buf, h, st=0):
            mine_rows = buf.at[own]
            for j in range(1, K):
                k2 = rm(k + j, K)
                remote(mine_rows, mine_rows, n.tpa_s.at[st, h, j], n.tpa_r.at[st, h, j], place(core * K + k2, g)).start()
            remote(mine_rows, mine_rows, n.tpa_s.at[st, h, 0], n.tpa_r.at[st, h, 0], sibling).start()

        def tp_finish(buf, h, st=0):
            def rows(c2, k2):
                return buf.at[pl.ds(mul(c2 * K + k2, RR), RR)]

            for j in range(1, K):
                k2 = rm(k - j + K, K)
                ref = rows(core, k2)
                wait(ref, n.tpa_r.at[st, h, j])
                remote(ref, ref, n.tpf_s.at[st, h, j], n.tpf_r.at[st, h, j], sibling).start()
            wait(rows(1 - core, k), n.tpa_r.at[st, h, 0])
            for j in range(1, K):
                wait(rows(1 - core, rm(k - j + K, K)), n.tpf_r.at[st, h, j])
            for j in range(K):
                wait(rows(core, k), n.tpa_s.at[st, h, j])
            for j in range(1, K):
                wait(rows(core, rm(k - j + K, K)), n.tpf_s.at[st, h, j])

        def rs_start(st, h, partial):
            n.rsas[st, h] = partial(mul(1 - core, HB)).astype(bf16)
            copy = remote(n.rsas.at[st, h], n.rsar.at[st, h], n.rsa_s.at[st, h], n.rsa_r.at[st, h], sibling)
            copy.start()
            n.rsp[h] = partial(mul(core, HB))
            wait(n.rsar.at[st, h], n.rsa_r.at[st, h])
            for j in range(1, K):
                k2 = rm(k + j, K)
                rows = pl.ds(mul(k2, RR), RR)
                n.rsbs[st, h, j] = (n.rsp[h, rows] + n.rsar[st, h, rows].astype(f32)).astype(bf16)
                remote(
                    n.rsbs.at[st, h, j],
                    n.rsbr.at[st, h, j],
                    n.rsb_s.at[st, h, j],
                    n.rsb_r.at[st, h, j],
                    place(core * K + k2, g),
                ).start()
            rows = pl.ds(mul(k, RR), RR)
            n.rsp[h, rows] = n.rsp[h, rows] + n.rsar[st, h, rows].astype(f32)
            wait(n.rsas.at[st, h], n.rsa_s.at[st, h])

        def rs_finish(st, h):
            acc = n.rsp[h, pl.ds(mul(k, RR), RR)]
            for j in range(1, K):
                wait(n.rsbr.at[st, h, j], n.rsb_r.at[st, h, j])
                acc = acc + n.rsbr[st, h, j].astype(f32)
            for j in range(1, K):
                wait(n.rsbs.at[st, h, j], n.rsb_s.at[st, h, j])
            return acc

        def halves(fn):
            if NH == 1:
                fn(0)
            else:
                pl.loop(0, NH)(fn)

        def weight(m, l, lo=0, hi=None):
            hi = mat_block[m][1] if hi is None else hi
            at = (l - half if m in DECODER_MATS else l,) + (slice(None),) * (NB + 1) + (slice(lo, hi),)
            return W[m][at].reshape((-1, hi - lo))

        def out_weight(m, l, c):
            parts = [W[m][(l - half if m in DECODER_MATS else l,) + group_bits(m, a * C + c)] for a in range(q)]
            return parts[0] if q == 1 else jnp.concatenate(parts, axis=0)

        def out_product(rows, m, l):
            return jnp.concatenate([dot(rows, out_weight(m, l, c), NN) for c in range(C)], axis=1)

        def out_product_back(grad, m, l):
            acc = None
            for c in range(C):
                term = dot(grad[:, c * cw : (c + 1) * cw], out_weight(m, l, c), NT)
                acc = term if acc is None else acc + term
            return acc

        def norm_row(l, row):
            return n.norms[l][row : row + 1, :]

        def ln_forward(t, h, value, gain, bias):
            centre = value - jnp.mean(value, axis=-1, keepdims=True)
            scale = lax.rsqrt(jnp.mean(centre * centre, axis=-1, keepdims=True) + EPSILON)
            z = centre * scale
            n.zs[t, h] = z.astype(bf16)
            n.rstd[t, h] = jnp.broadcast_to(scale, (RR, 128))
            return z * gain + bias

        def ln_backward(t, h, grad, l, gain_row, bias_row):
            z = n.zs[t, h].astype(f32)
            scale = n.rstd[t, h][:, :1]
            n.small[l, gain_row : gain_row + 1, :] += jnp.sum(grad * z, axis=0, keepdims=True)
            n.small[l, bias_row : bias_row + 1, :] += jnp.sum(grad, axis=0, keepdims=True)
            gz = grad * norm_row(l, gain_row)
            return scale * (
                gz - jnp.mean(gz, axis=-1, keepdims=True) - z * jnp.mean(gz * z, axis=-1, keepdims=True)
            )

        head_width = D // HEADS
        score_scale = 1.0 / math.sqrt(head_width)

        def allowed_of(h, causal):
            rows = lax.broadcasted_iota(jnp.int32, (R, R), 0)
            cols = lax.broadcasted_iota(jnp.int32, (R, R), 1)
            ok = (dv_vec(rows) == dv_vec(cols)) & (n.aux[h][1:2] > 0.5 if causal else n.aux[h][0:1] > 0.5)
            return ok & (cols <= rows) if causal else ok

        def dv_vec(v):
            return lax.div(v, jnp.full_like(v, p.seq))

        def head_lanes(head):
            lane = lax.broadcasted_iota(jnp.int32, (1, CW), 1)
            return (lane >= head * head_width) & (lane < (head + 1) * head_width)

        def only(value, head):
            return jnp.where(head_lanes(head), value, jnp.zeros_like(value))

        def probabilities(qs, ks, allowed, head):
            scores = dot(only(qs, head), ks, NT) * score_scale
            scores = jnp.where(allowed, scores, MASKED)
            e = jnp.exp(scores - jnp.max(scores, axis=-1, keepdims=True))
            return e / jnp.sum(e, axis=-1, keepdims=True)

        def attend(qs, ks, vs, allowed):
            out = jnp.zeros((R, CW), f32)
            for head in range(p.HPR):
                probs = probabilities(qs, ks, allowed, head)
                out = out + only(dot(probs.astype(bf16), vs, NN), head)
            return out.astype(bf16)

        def attend_back(qs, ks, vs, allowed, grad):
            gq = gk = gv = jnp.zeros((R, CW), f32)
            for head in range(p.HPR):
                probs = probabilities(qs, ks, allowed, head)
                gp = dot(only(grad, head), vs, NT)
                gs = (probs * (gp - jnp.sum(gp * probs, axis=-1, keepdims=True))).astype(bf16)
                gv = gv + only(dot(probs.astype(bf16), grad, TN), head)
                gq = gq + only(dot(gs, ks, NN), head)
                gk = gk + only(dot(gs, qs, TN), head)
            return (gq * score_scale).astype(bf16), (gk * score_scale).astype(bf16), gv.astype(bf16)

        def split3(value):
            return value[:, :CW], value[:, CW : 2 * CW], value[:, 2 * CW :]

        c0, c1 = math.sqrt(2.0 / math.pi), 0.044715

        def gelu(v):
            return 0.5 * v * (1.0 + jnp.tanh(c0 * (v + c1 * (v * v * v))))

        def gelu_slope(v):
            th = jnp.tanh(c0 * (v + c1 * (v * v * v)))
            return 0.5 * (1.0 + th) + 0.5 * v * (1.0 - th * th) * (c0 * (1.0 + 3.0 * c1 * v * v))

        def rows_home(src, dst, send, recv, l, h, act):
            here = (l == s) & (h == zl)

            @pl.when(here)
            def _():
                if act == "start":
                    local(src, dst.at[own], recv.at[r]).start()

            @pl.when(jnp.logical_not(here))
            def _():
                if act == "start":
                    to = (l, with_bit(PAIR_BIT, h) if tz == 2 else d)
                    remote(src, dst.at[own], send, recv.at[r], to).start()
                else:
                    wait(src, send)

        def self_forward(l, t, xi, causal, alpha, into):
            feed(t)
            ready(l, QKV, OUT)

            def first(h):
                n.qkv[l, h] = dot(n.xbuf[xi, h], weight(QKV, l), NN).astype(bf16)
                qs, ks, vs = split3(n.qkv[l, h])
                n.osv[l, h] = attend(qs, ks, vs, allowed_of(h, causal))
                rs_start(0, h, lambda row: out_product(n.osv[l, h, pl.ds(row, HB)], OUT, l))

            def second(h):
                value = alpha * n.xbuf[xi, h, own].astype(f32) + rs_finish(0, h)
                hidden = ln_forward(t, h, value, norm_row(l, 0), norm_row(l, 2))
                n.res[h] = hidden
                into[h, own] = hidden.astype(bf16)
                tp_start(into.at[h], h)

            halves(first)
            halves(second)

        def cross_forward(l, t):
            feed(t)
            ready(l, CQKV, COUT)
            ld = l - half

            def first(h):
                n.cqkv[ld, h, :, CW:] = dot(n.xbuf[half, h], weight(CQKV, l, CW), NN).astype(bf16)
                tp_finish(n.h1b.at[ld, h], h)
                n.cqkv[ld, h, :, :CW] = dot(n.h1b[ld, h], weight(CQKV, l, 0, CW), NN).astype(bf16)
                qs, ks, vs = split3(n.cqkv[ld, h])
                n.cosv[ld, h] = attend(qs, ks, vs, allowed_of(h, False))
                rs_start(0, h, lambda row: out_product(n.cosv[ld, h, pl.ds(row, HB)], COUT, l))

            def second(h):
                value = DECODER_ALPHA * n.res[h] + rs_finish(0, h)
                hidden = ln_forward(t, h, value, norm_row(l, 4), norm_row(l, 5))
                n.res[h] = hidden
                n.hb[l, h, own] = hidden.astype(bf16)
                tp_start(n.hb.at[l, h], h)

            halves(first)
            halves(second)

        def ffn_forward(l, t, xo, alpha):
            feed(t)
            ready(l, FIN)

            def first(h):
                tp_finish(n.hb.at[l, h], h)
                before = dot(n.hb[l, h], weight(FIN, l), NN)
                n.pre[l, h] = before.astype(bf16)
                n.actb[h] = gelu(before).astype(bf16)

            def send(h):
                rs_start(0, h, lambda row: dot(n.actb[h, pl.ds(row, HB)], weight(FOUT, l), NN))

            def second(h):
                value = alpha * n.res[h] + rs_finish(0, h)
                result = ln_forward(t, h, value, norm_row(l, 1), norm_row(l, 3))
                n.xbuf[xo, h, own] = result.astype(bf16)

                @pl.when(l < L - 1)
                def _():
                    tp_start(n.xbuf.at[xo, h], h, 1)

                @pl.when(l == L - 1)
                def _():
                    rows_home(n.xbuf.at[xo, h, own], n.out, n.fin_s.at[h], n.fin_r, L - 1, h, "start")

            def third(h):
                tp_finish(n.xbuf.at[xo, h], h, 1)

            halves(first)
            ready(l, FOUT)
            halves(send)
            halves(second)

            @pl.when(l < L - 1)
            def _():
                halves(third)

                @pl.when(s == l)
                def _():
                    local(n.xbuf.at[xo, zl], n.out, n.out_l.at[0]).start()

        for i in (2, 0):
            first_wait(i)
        for j in range(1, NS):
            wait(n.norms.at[rm(s - j + NS, NS)], n.norm_r.at[j])
        wait(n.norms.at[s], n.norm_s.at[0])
        n.small[...] = jnp.zeros_like(n.small)
        n.gmem[...] = jnp.zeros_like(n.gmem)

        @pl.loop(0, half)
        def _(l):
            self_forward(l, 2 * l, l, False, ENCODER_ALPHA, n.hb.at[l])
            ffn_forward(l, 2 * l + 1, l + 1, ENCODER_ALPHA)

        for i in (1, 3, 4):
            first_wait(i)

        @pl.loop(half, L)
        def _(l):
            t = 2 * half + 3 * (l - half)
            self_forward(l, t, l + 1, True, DECODER_ALPHA, n.h1b.at[l - half])
            cross_forward(l, t + 1)
            ffn_forward(l, t + 2, l + 2, DECODER_ALPHA)

        def gbuf(m, l):
            return G[m].at[rm(l, slots)]

        def gregion(m, l, fixed):
            return gbuf(m, l).at[tuple(fixed.get(b, slice(None)) for b in mat_bits[m])]

        def partner(j):
            b = back_steps[j - 1]
            return (s, with_bit(b, 1 - bit[b]))

        def gr_start(j, m, l):
            @pl.when(l != L - 1)
            def _():
                pl.semaphore_wait(n.credit.at[j - 1, m], 1)

            fixed = {b: bit[b] for b in back_steps[: j - 1]}
            fixed[back_steps[j - 1]] = 1 - bit[back_steps[j - 1]]
            remote(gregion(m, l, fixed), RB[m][j], n.gr_s.at[j - 1, m], n.gr_r.at[j - 1, m], partner(j)).start()

        def blocks_of(count):
            return [
                tuple((i >> b) & 1 for b in reversed(range(count))) for i in range(1 << count)
            ]

        def gr_finish(j, m, l):
            wait(RB[m][j], n.gr_r.at[j - 1, m])
            mine_part = gregion(m, l, {b: bit[b] for b in back_steps[:j]})
            for idx in blocks_of(len(mat_bits[m]) - j):
                value = mine_part[idx].astype(f32) + RB[m][j][idx].astype(f32)
                if j == nst:
                    ST[m][idx if idx else 0] = value.astype(bf16)
                else:
                    mine_part[idx] = value.astype(bf16)
            wait(RB[m][j], n.gr_s.at[j - 1, m])

            @pl.when(l != (half if m in DECODER_MATS else 0))
            def _():
                pl.semaphore_signal(n.credit.at[j - 1, m], inc=1, device_id=partner(j), device_id_type=MESH)

            if j < nst:
                gr_start(j + 1, m, l)
            else:
                for z in range(ST[m].shape[0]):
                    home(m, l, z, "start")

        def homes_wait(m, l):
            for z in range(ST[m].shape[0]):
                home(m, l, z, "wait")

        def home(m, l, z, act):
            src = ST[m].at[z]
            if m in (OUT, COUT):
                piece = rm(g, C)
                to = (l, r * q + dv(g, C))
                here = (l == s) & (to[1] == d)
                first = 3 * D if m == COUT else 0
                copies = [(src, H[m].at[:, pl.ds(pl.multiple_of(first + piece * cw, cw), cw)])]
                slot = piece
            else:
                to = (l, with_bit(PAIR_BIT, z) if tz == 2 else d)
                here = (l == s) & (zl == z) if tz == 2 else l == s
                copies = [(src.at[b], H[m].at[a]) for a, b in parts_of(m, r)]
                slot = r
            if act == "wait":
                wait(src, n.home_s.at[m, z])
                return

            @pl.when(here)
            def _():
                for a, b in copies:
                    local(a, b, n.home_s.at[m, z]).start()

            @pl.when(jnp.logical_not(here))
            def _():
                for a, b in copies:
                    remote(a, b, n.home_s.at[m, z], n.home_r.at[m, slot], to).start()

        def homes_wait(m, l):
            for z in range(ST[m].shape[0]):
                home(m, l, z, "wait")

        def process(u):
            if not lagged:
                return

            def old(kd, mats, l):
                for m in mats:
                    homes_wait(m, l)

            groups(T - 1 - (u - BEHIND[nst - 1] - 1), old)
            for j in range(1, nst + 1):

                def fn(kd, mats, l, j=j):
                    for m in mats:
                        gr_finish(j, m, l)

                groups(T - 1 - (u - BEHIND[j - 1]), fn)

        def send_grad(m, l):
            gr_start(1, m, l)
            if not lagged:
                for j in range(1, nst + 1):
                    gr_finish(j, m, l)
                homes_wait(m, l)

        def weight_grad(m, l, lefts, rights):
            rows, cols = mat_block[m]
            count = max(1, 128 // rows)
            tile = rows * count

            @pl.loop(0, ND // count)
            def _(i):
                span = pl.ds(mul(i, tile), tile)
                parts = []
                for left, right in zip(lefts, rights):
                    acc = None
                    for h in range(NH):
                        term = dot(left[h][:, span], right[h][...], TN)
                        acc = term if acc is None else acc + term
                    parts.append(acc)
                value = parts[0] if len(parts) == 1 else jnp.concatenate(parts, axis=1)
                value = value.astype(bf16)
                for e in range(count):
                    at = i * count + e
                    idx = tuple(rm(dv(at, 1 << b), 2) for b in reversed(range(NB)))
                    gbuf(m, l)[idx] = value[e * rows : (e + 1) * rows]

        def out_grad(m, l, left, right):
            for c in range(C):
                acc = None
                for h in range(NH):
                    term = dot(left[h][...], right[h][:, c * cw : (c + 1) * cw], TN)
                    acc = term if acc is None else acc + term
                acc = acc.astype(bf16)
                for a in range(q):
                    gbuf(m, l)[group_bits(m, a * C + c)] = acc[a * p.rb : (a + 1) * p.rb]

        def each(ref):
            return [ref.at[h] for h in range(NH)]

        def branch_grad(t, l, u, gain_row, bias_row):
            gag = n.gag.at[rm(u, 2)]

            def fn(h):
                grad = ln_backward(t, h, n.gy[h], l, gain_row, bias_row)
                n.res[h] = grad
                gag[h, own] = grad.astype(bf16)
                tp_start(gag.at[h], h)

            halves(fn)
            return gag

        def ffn_backward(l, t, u, alpha):
            gag = branch_grad(t, l, u, 1, 3)

            def first(h):
                tp_finish(gag.at[h], h)
                before = n.pre[l, h].astype(f32)
                gact = dot(gag[h], weight(FOUT, l), NT)
                n.gpre[h] = (gact * gelu_slope(before)).astype(bf16)
                rs_start(0, h, lambda row: dot(n.gpre[h, pl.ds(row, HB)], weight(FIN, l), NT))
                n.actb[h] = gelu(before).astype(bf16)

            halves(first)
            weight_grad(FOUT, l, [each(n.actb)], [each(gag)])
            process(u)
            send_grad(FOUT, l)
            weight_grad(FIN, l, [each(n.hb.at[l])], [each(n.gpre)])
            send_grad(FIN, l)

            def second(h):
                n.gy[h] = alpha * n.res[h] + rs_finish(0, h)

            halves(second)

        def cross_backward(l, t, u):
            gag = branch_grad(t, l, u, 4, 5)
            ld = l - half

            def first(h):
                tp_finish(gag.at[h], h)
                grad = out_product_back(gag.at[h], COUT, l).astype(bf16)
                qs, ks, vs = split3(n.cqkv[ld, h])
                gq, gk, gv = attend_back(qs, ks, vs, allowed_of(h, False), grad)
                n.gqkv[h, :, :CW] = gq
                n.gqkv[h, :, CW : 2 * CW] = gk
                n.gqkv[h, :, 2 * CW :] = gv
                rs_start(
                    0, h, lambda row: dot(n.gqkv[h, pl.ds(row, HB), :CW], weight(CQKV, l, 0, CW), NT)
                )
                n.gmem[h] += dot(n.gqkv[h, :, CW:], weight(CQKV, l, CW), NT)

            halves(first)
            out_grad(COUT, l, each(n.cosv.at[ld]), each(gag))
            process(u)
            send_grad(COUT, l)
            weight_grad(
                CQKV,
                l,
                [each(n.h1b.at[ld]), each(n.xbuf.at[half])],
                [
                    [n.gqkv.at[h, :, pl.ds(0, CW)] for h in range(NH)],
                    [n.gqkv.at[h, :, pl.ds(CW, 2 * CW)] for h in range(NH)],
                ],
            )
            send_grad(CQKV, l)

            def second(h):
                n.gy[h] = DECODER_ALPHA * n.res[h] + rs_finish(0, h)

            halves(second)

        def sig_copy(l, h, act):
            rows_home(n.gxo.at[l, h], n.sig, n.sig_s.at[l, h], n.sig_r, l, h, act)

        def self_backward(l, t, u, xi, causal, alpha):
            gag = branch_grad(t, l, u, 0, 2)

            def first(h):
                tp_finish(gag.at[h], h)
                grad = out_product_back(gag.at[h], OUT, l).astype(bf16)
                qs, ks, vs = split3(n.qkv[l, h])
                gq, gk, gv = attend_back(qs, ks, vs, allowed_of(h, causal), grad)
                n.gqkv[h, :, :CW] = gq
                n.gqkv[h, :, CW : 2 * CW] = gk
                n.gqkv[h, :, 2 * CW :] = gv
                rs_start(0, h, lambda row: dot(n.gqkv[h, pl.ds(row, HB)], weight(QKV, l), NT))

            halves(first)
            out_grad(OUT, l, each(n.osv.at[l]), each(gag))
            process(u)
            send_grad(OUT, l)
            weight_grad(QKV, l, [each(n.xbuf.at[xi])], [each(n.gqkv)])
            send_grad(QKV, l)

            def second(h):
                grad = (alpha * n.res[h] + rs_finish(0, h)).astype(bf16)
                n.gxo[l, h] = grad
                n.gy[h] = grad.astype(f32)
                sig_copy(l, h, "start")

            halves(second)

        def seed(h):
            n.gy[h] = n.cotb[h].astype(f32)

        halves(seed)

        @pl.loop(0, LD)
        def _(i):
            l = L - 1 - i
            t = 2 * half + 3 * (l - half)
            ffn_backward(l, t + 2, 3 * i, DECODER_ALPHA)
            cross_backward(l, t + 1, 3 * i + 1)
            self_backward(l, t, 3 * i + 2, l + 1, True, DECODER_ALPHA)

        def directions(h):
            column = n.dirw[h, dv(r * RR, p.seq)][:, :1]
            rows = column * jnp.sum(n.gy[h], axis=0, keepdims=True)
            for sec in range(NS):
                lo = sec * p.dir_rows
                n.small[sec, 8 : 8 + p.dir_rows, :] += rows[lo : lo + p.dir_rows]

        halves(directions)

        def memory_first(h):
            rs_start(1, h, lambda row: n.gmem[h, pl.ds(row, HB)])

        def memory_second(h):
            n.gy[h] = rs_finish(1, h).astype(bf16).astype(f32)

        halves(memory_first)
        halves(memory_second)

        @pl.loop(0, half)
        def _(i):
            l = half - 1 - i
            u = 3 * LD + 2 * i
            ffn_backward(l, 2 * l + 1, u, ENCODER_ALPHA)
            self_backward(l, 2 * l, u + 1, l, False, ENCODER_ALPHA)

        process(T)

        for rank in range(TPN):
            for g2 in range(NU):
                sec, d2 = place(rank, g2)
                lo = d2 * p.cols
                tile, lane = divmod(g2 * p.cols, 128)
                n.sm1[rank, tile, :, lane : lane + p.cols] = n.small[sec, :, lo : lo + p.cols]
        for j in range(1, TPN):
            to = rm(r + j, TPN)
            remote(n.sm1.at[to], n.sm1r.at[j], n.sm1_s.at[j], n.sm1_rs.at[j], place(to, g)).start()

        if lagged:

            @pl.loop(1, BEHIND[nst - 1] + 1)
            def _(i):
                process(T + i)

        total_small = n.sm1[r]
        for j in range(1, TPN):
            wait(n.sm1r.at[j], n.sm1_rs.at[j])
            total_small = total_small + n.sm1r[j]
        for g2 in range(NU):
            tile, lane = divmod(g2 * p.cols, 128)
            n.sm2[g2, :, : p.cols] = total_small[tile, :, lane : lane + p.cols]
        for j in range(1, NU):
            to = rm(g + j, NU)
            remote(n.sm2.at[to], n.sm2r.at[j], n.sm2_s.at[j], n.sm2_rs.at[j], place(r, to)).start()
        mine_small = n.sm2[g]
        for j in range(1, NU):
            wait(n.sm2r.at[j], n.sm2_rs.at[j])
            mine_small = mine_small + n.sm2r[j]
        n.smo[...] = mine_small
        local(n.smo, n.smout, n.smo_l.at[0]).start()
        wait(n.smo, n.smo_l.at[0])

        def home_wait(m):
            for j in range(1, TPN):
                rank = rm(r + j, TPN)
                wait(ST[m].at[0], n.home_r.at[m, rank])

        def home_wait_out(m):
            for c, span, group, rank, here in out_pieces(m):

                @pl.when(jnp.logical_not(here))
                def _():
                    wait(H[m].at[:, span], n.home_r.at[m, c])

        for m in (QKV, FIN, FOUT):
            home_wait(m)
        home_wait_out(OUT)

        @pl.when(s >= half)
        def _():
            home_wait(CQKV)
            home_wait_out(COUT)

        for rank in range(TPN):
            wait(n.sig.at[pl.ds(rank * RR, RR)], n.sig_r.at[rank])
        @pl.when(s < L - 1)
        def _():
            wait(n.out, n.out_l.at[0])

        @pl.when(s == L - 1)
        def _():
            for rank in range(TPN):
                wait(n.out.at[pl.ds(rank * RR, RR)], n.fin_r.at[rank])

        for h in range(NH):
            rows_home(n.xbuf.at[L + 1, h, own], n.out, n.fin_s.at[h], n.fin_r, L - 1, h, "wait")
        for l in range(L):
            for h in range(NH):
                sig_copy(l, h, "wait")
        for j in range(1, TPN):
            wait(n.sm1.at[0], n.sm1_s.at[j])
        for j in range(1, NU):
            wait(n.sm2.at[0], n.sm2_s.at[j])
        for j in range(1, NS):
            wait(n.norms.at[0], n.norm_s.at[j])
        for j in range(1, TPN):
            for m in (QKV, FIN, FOUT):
                wait(ST[m].at[0], n.a2a_s.at[m, j])

        @pl.when(s >= half)
        def _():
            for j in range(1, TPN):
                wait(ST[CQKV].at[0], n.a2a_s.at[CQKV, j])

        for m in (OUT, COUT):
            for c, span, group, rank, here in out_pieces(m):
                sends = jnp.logical_not(here) if m == OUT else jnp.logical_not(here) & (s >= half)

                @pl.when(sends)
                def _():
                    wait(ST[m].at[0], n.wo_s.at[m - OUT, c])

        @pl.loop(0, L)
        def _(l):
            for j in range(nst):
                for m in mat_block:
                    if m not in DECODER_MATS:
                        wait(ag_region(j, m, l, False), n.ag_s.at[j, m, l])

                @pl.when(l >= half)
                def _():
                    for m in DECODER_MATS:
                        wait(ag_region(j, m, l, False), n.ag_s.at[j, m, l])

    def sd(*shape, dtype=bf16):
        return jax.ShapeDtypeStruct(shape, dtype)

    def blocks(m, lead):
        return sd(lead, *mat_block[m])

    outs = [
        sd(R, D),
        sd(R, D),
        sd(p.rb, 3 * D),
        blocks(FIN, TPN),
        blocks(FOUT, TPN),
        sd(p.rb, 4 * D),
        sd(p.rb, D),
        sd(16, 128, dtype=f32),
    ]
    anywhere = pl.BlockSpec(memory_space=pl.ANY)
    return pl.pallas_call(
        kernel,
        out_shape=outs,
        in_specs=[anywhere] * len(in_names),
        out_specs=[anywhere] * len(out_names),
        scratch_shapes=list(scratch.values()),
        compiler_params=pltpu.CompilerParams(
            collective_id=0, has_side_effects=True, vmem_limit_bytes=64 * 1024 * 1024 - 64 * 1024
        ),
    )


def solution(mesh):
    def body(
        source,
        target,
        directions,
        source_lengths,
        target_lengths,
        attn_in,
        attn_out,
        ffn_in,
        ffn_out,
        cross_weight,
        norm_gain,
        norm_bias,
        cross_norm,
        dir_table,
        cotangent,
    ):
        pairs, seq, width = source.shape
        p = make_plan(
            mesh.shape["section"], mesh.shape["dp"], pairs, seq, width, ffn_in.shape[2], dir_table.shape[0]
        )
        section = lax.axis_index("section")
        routing = (directions[:, None] == jnp.arange(p.NDIR)[None, :]).astype(f32)
        rows = jnp.dot(routing, dir_table, precision=lax.Precision.HIGHEST)
        x2 = (target.astype(f32) + rows[:, None, :]).astype(bf16).reshape(p.R, width)
        positions = jnp.arange(seq)
        valid = [(positions[None, :] < lens[:, None]).astype(f32).reshape(1, p.R) for lens in (source_lengths, target_lengths)]
        aux = jnp.concatenate(valid + [jnp.zeros((6, p.R), f32)], axis=0)
        dirw = jnp.broadcast_to(routing[:, :, None], (pairs, p.NDIR, 128))
        norms = jnp.concatenate(
            (norm_gain[0], norm_bias[0], cross_norm[0], jnp.zeros((2, width), bf16)), axis=0
        ).astype(f32)
        ai = ffn_in[0].reshape(p.rb, p.ND, p.TPN, p.fb).transpose(2, 0, 1, 3).reshape(p.TPN, p.rb, p.FB)
        af = ffn_out[0].reshape(p.TPN, p.fb, width)
        out, sig, hq, hi, hf, hc, hwo, small = build(p)(
            source.reshape(p.R, width),
            x2,
            cotangent.reshape(p.R, width),
            aux,
            dirw,
            norms,
            attn_in[0],
            ai,
            af,
            cross_weight[0],
            attn_out[0],
        )
        decoder = section >= p.half

        g_in = hi.reshape(p.TPN, p.rb, p.ND, p.fb).transpose(1, 2, 0, 3).reshape(1, p.rb, p.FF).astype(f32)
        g_out = hf.reshape(1, p.TPN * p.fb, width).astype(f32)
        g_wo = hwo.astype(f32)[None]
        g_cross = jnp.where(decoder, hc.astype(f32), jnp.zeros(hc.shape, f32))[None]
        small = small[:, : p.cols]
        return (
            out.reshape(1, pairs, seq, width),
            sig.reshape(1, pairs, seq, width),
            hq.astype(f32)[None],
            g_wo,
            g_in,
            g_out,
            g_cross,
            small[None, 0:2],
            small[None, 2:4],
            small[None, 4:6],
            small[8 : 8 + p.dir_rows],
        )

    sharded = P("section", "dp", None)
    return jax.shard_map(
        body,
        mesh=mesh,
        in_specs=(
            P("dp", None, None),
            P("dp", None, None),
            P("dp"),
            P("dp"),
            P("dp"),
            sharded,
            sharded,
            sharded,
            sharded,
            sharded,
            P("section", None, None),
            P("section", None, None),
            P("section", None, None),
            P(),
            P("dp", None, None),
        ),
        out_specs=(
            P("section", "dp", None, None),
            P("section", "dp", None, None),
            sharded,
            sharded,
            sharded,
            sharded,
            sharded,
            P("section", None, "dp"),
            P("section", None, "dp"),
            P("section", None, "dp"),
            P("section", "dp"),
        ),
        check_vma=False,
    )
```
